128 devices in a mesh: facet: 8 (over x_lo, y), bl: 8 (over z, core), chan: 2 (over x_hi).
Axes of the slice: x: 4 (x_hi: 2, x_lo: 2; x = x_hi * 2 + x_lo), y: 4, z: 4, core: 2. Of those that a mesh axis runs over, the one named last changes fastest.
Arguments:
- visibilities: bfloat16 [512, 8, 2, 128], P(('facet', 'bl'), 'chan'), may hold values from -6 to 6
- coords: bfloat16 [512, 2, 128], P(('facet', 'bl')), may hold values from 4 to 124
- plane_index: int32 [512], P(('facet', 'bl')), may hold values from 0 to 63, as said below
- block_group: int32 [512, 1], P(('facet', 'bl')), may hold values from 0 to 7, as said below
- offsets: int32 [8, 8, 2], replicated, may hold values from 0 to 7
- facet_centre: float32 [8, 2], replicated, may hold values from -8 to 8
- tables: bfloat16 [64, 2, 128, 2, 128], P(('facet', 'bl')), may hold values from -0.5 to 0.5
- antenna_gain: float32 [8, 2, 128], P('bl'), may hold values from 0.1 to 1.9
Outputs:
- subgrids: float32 [8, 8, 128, 2, 128], P('facet', 'bl', 'chan')
The draws below stay inside these ranges and needn't reach their ends.
Inputs may be any that keep to these rules, and one draw needn't show every extreme that they name: `block_group`: among the 8 blocks of one device at most 2 name the same baseline group, and on every device some group is named by exactly 2 of them. `plane_index`: A block whose baseline group is g names a w-plane p with p modulo 8 equal to g or to (g + 7) modulo 8.
All inputs are finite; a program needn't handle non-finite values.
Results may differ from the reference program's by a relative error of at most 0.0054.
Values may be sent and summed in bfloat16 or wider, within the bound.
A program may use at most 64 MiB of HBM per device.

```python
import math
import jax
import jax.numpy as jnp
from jax import lax

SU = 128
BLK = 128
CH = 8
NB_DEV = 8
CAP = 2
FACETS = 8
GROUPS = 8
NB = 512
P_SIZE = 64


def group_rows(key):
    folded = jax.random.fold_in(key, 101)
    second_key = jax.random.fold_in(folded, 1)
    third_key = jax.random.fold_in(folded, 2)
    device_count = NB // NB_DEV
    slot_count = GROUPS * CAP
    chosen = (jnp.arange(device_count, dtype=jnp.int32) % GROUPS)[:, None]
    slot_ids = jnp.arange(slot_count, dtype=jnp.int32)
    jitter = jax.random.randint(second_key, (device_count, slot_count), 0, 1024)
    scores = jitter * slot_count + slot_ids[None, :] + jnp.where(slot_ids[None, :] // CAP == chosen, 0, 1024 * slot_count)
    ranked = jnp.argsort(scores, axis=1)
    picked = (ranked[:, :NB_DEV] // CAP).astype(jnp.int32)
    mixing = jax.random.randint(third_key, (device_count, NB_DEV), 0, 1024) * NB_DEV + jnp.arange(NB_DEV, dtype=jnp.int32)[None, :]
    shuffle = jnp.argsort(mixing, axis=1)
    result_rows = jnp.take_along_axis(picked, shuffle, axis=1)
    return result_rows.reshape(NB).astype(jnp.int32)


def draw_block_group(key, part):
    return group_rows(key)[:, None]


def draw_plane_index(key, part):
    group_ids = group_rows(key)
    folded = jax.random.fold_in(key, 202)
    first_key, second_key, third_key = jax.random.split(folded, 3)
    draw_a = jax.random.randint(first_key, (NB,), 0, FACETS)
    draw_b = jax.random.randint(second_key, (NB,), 0, 2 * FACETS)
    depth_level = jnp.minimum(draw_a, draw_b)
    advance = jax.random.randint(third_key, (NB,), 0, 2)
    normal_plane = depth_level * GROUPS + (group_ids + GROUPS - advance) % GROUPS
    device_count = NB // NB_DEV
    device_ids = jnp.arange(NB, dtype=jnp.int32) // NB_DEV
    own = (group_ids == device_ids % GROUPS).astype(jnp.int32).reshape(device_count, NB_DEV)
    first_own = ((jnp.cumsum(own, axis=1) == 1) & (own == 1)).reshape(NB)
    special = (device_ids + device_count - 1) % device_count
    return jnp.where(first_own, special, normal_plane).astype(jnp.int32)


def plant(result, stream_key, low, largest):
    longest = result.shape.index(max(result.shape))
    spots = []
    for shift in (0, 1):
        where = [jax.random.randint(jax.random.fold_in(stream_key, axis), (), 0, length) for axis, length in enumerate(result.shape)]
        where[longest] = (where[longest] + shift) % result.shape[longest]
        spots.append(tuple(where))
    return result.at[spots[0]].set(low).at[spots[1]].set(largest)


def block_levels(stream_key, dims, shards, least, top_value):
    loudness = 1.0
    for axis_at, parts in shards:
        draws = jax.random.uniform(jax.random.fold_in(jax.random.fold_in(stream_key, 6), axis_at), (parts,), jnp.float32, least / len(shards), top_value / len(shards))
        loudness = loudness * jnp.repeat(jnp.exp(draws), dims[axis_at] // parts).reshape((-1,) + (1,) * (len(dims) - 1 - axis_at))
    return loudness


def centred(own_key, extent, deviation, reach, shards=(), kind=jnp.bfloat16):
    values = deviation * jax.random.normal(own_key, extent, jnp.float32)
    if shards:
        values = values * block_levels(own_key, extent, shards, -0.22, 0.18)
    return jnp.clip(values, -reach, reach).astype(kind)


def setup_inputs(seed: int = 0) -> dict:
    arg_keys = jax.random.split(jax.random.key(seed), 9)
    return {
        "visibilities": centred(arg_keys[0], (NB, CH, 2, BLK), 1.0, 6.0, ((0, 64), (1, 2))),
        "coords": jnp.clip(4.0 + 120.0 * jax.random.uniform(arg_keys[1], (NB, 2, BLK), jnp.float32) ** block_levels(arg_keys[1], (NB, 2, BLK), ((0, 64),), -0.2, 0.2), 4.0, 124.0).astype(jnp.bfloat16),
        "plane_index": draw_plane_index(jax.random.fold_in(arg_keys[8], 71), 0),
        "block_group": draw_block_group(jax.random.fold_in(arg_keys[8], 71), 0),
        "offsets": plant(jax.random.randint(arg_keys[4], (FACETS, GROUPS, 2), 0, 8), jax.random.fold_in(arg_keys[4], 1), 0, 7).astype(jnp.int32),
        "facet_centre": jnp.clip(jax.random.uniform(arg_keys[5], (FACETS, 2), jnp.float32, -8.0, 8.0), -8.0, 8.0),
        "tables": centred(arg_keys[6], (P_SIZE, 2, SU, 2, SU), SU ** -0.5, 0.5, ((0, 64),)),
        "antenna_gain": jnp.clip(1.0 + 0.18 * jax.random.normal(arg_keys[7], (GROUPS, 2, SU), jnp.float32), 0.1, 1.9),
    }


kernel_spread = 1.5

def channel_scale(count, first):
    index = (first + jnp.arange(count, dtype=jnp.int32)).astype(jnp.float32)
    return 1.0 + 0.01 * (index - 0.5 * (CH - 1))

def grid_block(samples, place, kernel, shift, centre, scale):
    cells = jnp.arange(SU, dtype=jnp.int32).astype(jnp.float32)
    along_u = place[0].astype(jnp.float32)
    along_v = place[1].astype(jnp.float32)

    def profile(position, offset):
        spot = scale[:, None] * position[None, :] - offset
        apart = spot[:, :, None] - cells
        return jnp.exp(-apart * apart / (2.0 * kernel_spread * kernel_spread)).astype(jnp.bfloat16).reshape(CH * BLK, SU)
    spread_u = jnp.dot(profile(along_u, shift[0]), kernel[0].reshape(SU, 2 * SU), preferred_element_type=jnp.float32)
    spread_v = jnp.dot(profile(along_v, shift[1]), kernel[1].reshape(SU, 2 * SU), preferred_element_type=jnp.float32).astype(jnp.bfloat16)
    phase = 2.0 * math.pi / SU * (scale[:, None] * (along_u * centre[0] + along_v * centre[1])[None, :])
    phase = phase.reshape(CH * BLK, 1)
    real_part = samples[:, 0].astype(jnp.float32).reshape(CH * BLK, 1)
    imag_part = samples[:, 1].astype(jnp.float32).reshape(CH * BLK, 1)
    cosine = jnp.cos(phase)
    sine = jnp.sin(phase)
    turned_real = real_part * cosine - imag_part * sine
    turned_imag = real_part * sine + imag_part * cosine
    weighted_real = spread_u[:, :SU] * turned_real - spread_u[:, SU:] * turned_imag
    weighted_imag = spread_u[:, :SU] * turned_imag + spread_u[:, SU:] * turned_real
    weighted = jnp.concatenate([weighted_real, weighted_imag], axis=1).astype(jnp.bfloat16)
    product = jnp.dot(weighted.T, spread_v, preferred_element_type=jnp.float32)
    grid_real = product[:SU, :SU] - product[SU:, SU:]
    grid_imag = product[:SU, SU:] + product[SU:, :SU]
    return jnp.stack([grid_real, grid_imag], axis=1)

def reference(visibilities, coords, plane_index, block_group, offsets, facet_centre, tables, antenna_gain):
    scale = channel_scale(CH, 0)
    owners = block_group[:, 0]

    def one_facet(facet):
        shifts = offsets[facet].astype(jnp.float32)
        centre = facet_centre[facet]

        def step(carry, block):
            owner = owners[block]
            kernel = tables[plane_index[block]]
            part = grid_block(visibilities[block], coords[block], kernel, shifts[owner], centre, scale)
            return (carry.at[owner].add(part), None)
        start = jnp.zeros((GROUPS, SU, 2, SU), jnp.float32)
        total, _ = lax.scan(step, start, jnp.arange(NB, dtype=jnp.int32))
        return total
    raw = lax.map(one_facet, jnp.arange(FACETS, dtype=jnp.int32))
    norm = SU / math.sqrt(BLK * NB_DEV * FACETS * CH)
    gains = antenna_gain[:, 0][:, :, None, None] * antenna_gain[:, 1][:, None, None, :]
    return raw * gains[None] * norm
```

```python
import math

import jax
import jax.numpy as jnp
from jax import lax
from jax.experimental import pallas as pl
from jax.experimental.pallas import tpu as pltpu
from jax.sharding import PartitionSpec as P

SU = 128
CH = 8
SPREAD = 1.5
ROOT = math.sqrt(math.log2(math.e) / (2.0 * SPREAD * SPREAD))
MESH = pl.DeviceIdType.MESH
F32 = jnp.float32
BF16 = jnp.bfloat16
TILES = 11
STEP = 4


def route_kernel(
    pack_ref, group_ref, tab_ref, blocks_ref, tabs_ref,
    send, recv, stage, a_send, a_recv, b_send, b_recv, t_send, t_recv, own_sem,
):
    f = lax.axis_index("facet")
    g = lax.axis_index("bl")
    c = lax.axis_index("chan")
    before = lax.rem(g + 7, 8)
    after = lax.rem(g + 1, 8)

    barrier = pltpu.get_barrier_semaphore()
    for d in range(1, 8):
        pl.semaphore_signal(
            barrier, inc=1, device_id=(f, lax.rem(g + d, 8), c), device_id_type=MESH
        )
        pl.semaphore_signal(
            barrier, inc=1, device_id=(lax.rem(f + d, 8), g, c), device_id_type=MESH
        )
        pl.semaphore_signal(
            barrier, inc=1, device_id=(lax.rem(f + d, 8), before, c), device_id_type=MESH
        )

    labels = [group_ref[n, 0] for n in range(8)]

    def build(group, carry):
        zero = jnp.int32(0)
        i0, i1, n0, n1 = zero, zero, zero, zero
        for n in reversed(range(8)):
            match = labels[n] == group
            i1 = jnp.where(match, i0, i1)
            n1 = jnp.where(match, n0, n1)
            i0 = jnp.where(match, n, i0)
            n0 = jnp.where(match, 1, n0)
        one = pack_ref[i0].astype(F32) * n0.astype(F32)
        two = pack_ref[i1].astype(F32) * n1.astype(F32)
        send[group, 0] = jnp.concatenate([one[:8], two[:8]], axis=0).astype(BF16)
        send[group, 1] = jnp.concatenate([one[8:], two[8:]], axis=0).astype(BF16)
        return carry

    lax.fori_loop(0, 8, build, 0)
    pl.semaphore_wait(barrier, 21)

    def copy_a(d, peer):
        return pltpu.make_async_remote_copy(
            src_ref=send.at[peer], dst_ref=recv.at[g], send_sem=a_send.at[d],
            recv_sem=a_recv.at[g], device_id=(f, peer, c), device_id_type=MESH,
        )

    def copy_t(d, shift):
        facet = lax.rem(f + d, 8)
        return pltpu.make_async_remote_copy(
            src_ref=tab_ref, dst_ref=tabs_ref.at[f, shift], send_sem=t_send.at[shift, d],
            recv_sem=t_recv.at[shift, f], device_id=(facet, after if shift else g, c),
            device_id_type=MESH,
        )

    def copy_b(d):
        return pltpu.make_async_remote_copy(
            src_ref=stage, dst_ref=blocks_ref.at[f], send_sem=b_send.at[d],
            recv_sem=b_recv.at[f], device_id=(lax.rem(f + d, 8), g, c), device_id_type=MESH,
        )

    for d in range(1, 8):
        copy_a(d, lax.rem(g + d, 8)).start()
    for d in range(8):
        for shift in (0, 1):
            if d or shift:
                copy_t(d, shift).start()
    own_tab = pltpu.make_async_copy(tab_ref, tabs_ref.at[f, 0], own_sem.at[0])
    own_tab.start()
    recv[g] = send[g]
    for d in range(1, 8):
        peer = lax.rem(g + d, 8)
        pltpu.make_async_remote_copy(
            src_ref=send.at[peer], dst_ref=recv.at[peer], send_sem=a_send.at[d],
            recv_sem=a_recv.at[peer], device_id=(f, peer, c), device_id_type=MESH,
        ).wait_recv()

    rows = lax.broadcasted_iota(jnp.int32, (16, SU), 0)
    extra = [jnp.zeros((16, SU), F32) for _ in range(3)]
    for b in range(8):
        stage[b] = recv[b, 0]
        misc = recv[b, 1].astype(F32)
        for k in range(2):
            here = rows == 2 * b + k
            for e in range(3):
                line = 8 * k + e
                extra[e] = jnp.where(here, misc[line : line + 1], extra[e])
    for e in range(3):
        stage[8 + e] = extra[e].astype(BF16)
    for d in range(1, 8):
        copy_b(d).start()
    own_blocks = pltpu.make_async_copy(stage, blocks_ref.at[f], own_sem.at[1])
    own_blocks.start()
    for d in range(1, 8):
        peer = lax.rem(f + d, 8)
        pltpu.make_async_remote_copy(
            src_ref=stage, dst_ref=blocks_ref.at[peer], send_sem=b_send.at[d],
            recv_sem=b_recv.at[peer], device_id=(peer, g, c), device_id_type=MESH,
        ).wait_recv()
    for d in range(8):
        peer = lax.rem(f + d, 8)
        for shift in (0, 1):
            if d or shift:
                pltpu.make_async_remote_copy(
                    src_ref=tab_ref, dst_ref=tabs_ref.at[peer, shift],
                    send_sem=t_send.at[shift, d], recv_sem=t_recv.at[shift, peer],
                    device_id=(peer, after if shift else g, c), device_id_type=MESH,
                ).wait_recv()
    own_tab.wait()
    own_blocks.wait()
    for d in range(1, 8):
        copy_a(d, lax.rem(g + d, 8)).wait_send()
        copy_b(d).wait_send()
    for d in range(8):
        for shift in (0, 1):
            if d or shift:
                copy_t(d, shift).wait_send()


def sine_of_turns(turns):
    part = turns - jnp.floor(turns + 0.5)
    part = jnp.maximum(jnp.minimum(part, 0.5 - part), -0.5 - part)
    angle = part * (2.0 * math.pi)
    square = angle * angle
    total = jnp.full_like(angle, -1.0 / math.factorial(11))
    for power in (9, 7, 5, 3, 1):
        sign = 1.0 if power % 4 == 1 else -1.0
        total = total * square + sign / math.factorial(power)
    return total * angle


def grid_kernel(
    blocks_ref, offsets_ref, centre_ref, tabs_hbm, keep_ref, give_ref,
    vis, line_u, line_v, order_v, order, turned, spots, planes, tabs, raw, sems,
):
    f = lax.axis_index("facet")
    g = lax.axis_index("bl")
    c = lax.axis_index("chan")
    fetch = pltpu.make_async_copy(tabs_hbm, tabs, sems.at[0])
    fetch.start()

    sub = lax.broadcasted_iota(jnp.int32, (SU, SU), 0)
    lane = lax.broadcasted_iota(jnp.int32, (SU, SU), 1)
    label = jnp.concatenate([blocks_ref[i, 10] for i in range(8)], axis=0)
    label = label.astype(F32).astype(jnp.int32) - 1
    number = (label >> 3) * 2 + jnp.where((label & 7) == g, 0, 1)
    number = jnp.where(label >= 0, number, 16).astype(F32)
    across = number.T
    ahead = (across < number) | ((across == number) & (lane < sub))
    place = jnp.sum(jnp.where(ahead, 1.0, 0.0), axis=1, keepdims=True)
    hit = place == lane.astype(F32)
    lines = [
        jnp.sum(jnp.where(hit, sub.astype(F32), 0.0), axis=0, keepdims=True),
        jnp.sum(jnp.where(hit, number, 0.0), axis=0, keepdims=True),
        jnp.sum(jnp.where(number < 16.0, 1.0, 0.0), axis=0, keepdims=True),
        jnp.zeros((5, SU), F32),
    ]
    order_v[...] = jnp.concatenate(lines, axis=0).astype(jnp.int32)
    orders = pltpu.make_async_copy(order_v, order, sems.at[1])
    orders.start()

    for i in range(8):
        line_u[16 * i : 16 * i + 16] = blocks_ref[i, 8].astype(F32)
        line_v[16 * i : 16 * i + 16] = blocks_ref[i, 9].astype(F32)
        for b in range(8):
            both = blocks_ref[i, b].astype(F32)
            vis[16 * i + 2 * b] = both[:8]
            vis[16 * i + 2 * b + 1] = both[8:]
    planes[...] = jnp.zeros_like(planes)
    orders.wait()
    steps = (order[2, 0] + STEP - 1) // STEP

    off_u = offsets_ref[f, g, 0].astype(F32)
    off_v = offsets_ref[f, g, 1].astype(F32)
    dir_l = centre_ref[f, 0]
    dir_m = centre_ref[f, 1]
    row = lax.broadcasted_iota(jnp.int32, (8, SU), 0)
    upper = row < 4
    channel = (c * 4 + (row & 3)).astype(F32)
    scale = 1.0 + 0.01 * (channel - 0.5 * (CH - 1))

    def prepare(step, carry):
        for q in range(STEP):
            at = step * STEP + q
            slot = order[0, at]
            u = line_u[pl.ds(slot, 1), :]
            v = line_v[pl.ds(slot, 1), :]
            along = jnp.where(upper, scale * u - off_u, scale * v - off_v)
            spots[at] = along * ROOT
            turns = (scale * (u * dir_l + v * dir_m)) * (1.0 / SU)
            turns = turns - jnp.floor(turns + 0.5)
            wave = sine_of_turns(turns + jnp.where(upper, 0.25, 0.0))
            data = vis[slot]
            straight = data * wave
            crossed = data * pltpu.roll(wave, 4, 0)
            turned[at] = jnp.where(
                upper, straight - pltpu.roll(straight, 4, 0), crossed + pltpu.roll(crossed, 4, 0)
            )
        return carry

    lax.fori_loop(0, steps, prepare, 0)

    cells = sub.astype(F32) * ROOT

    def profile(line):
        apart = line - cells
        return jnp.exp2(-(apart * apart)).astype(BF16)

    def gather(step, carry):
        for q in range(STEP):
            at = step * STEP + q
            along_u, real, imag = [], [], []
            for ch in range(4):
                along_u.append(profile(spots[at, ch : ch + 1, :]))
                along_v = profile(spots[at, 4 + ch : 5 + ch, :])
                real.append(along_v * turned[at, ch : ch + 1, :].astype(BF16))
                imag.append(along_v * turned[at, 4 + ch : 5 + ch, :].astype(BF16))
            left = jnp.concatenate(along_u, axis=1)
            right = jnp.concatenate(
                [jnp.concatenate(real, axis=1), jnp.concatenate(imag, axis=1)], axis=0
            )
            planes[order[1, at]] += lax.dot_general(
                left, right, (((1,), (1,)), ((), ())), preferred_element_type=F32
            )
        return carry

    lax.fori_loop(0, steps, gather, 0)
    fetch.wait()

    def turn(re, im):
        return jnp.concatenate(
            [jnp.concatenate([re, im], axis=1), jnp.concatenate([-im, re], axis=1)], axis=0
        )

    total = jnp.zeros((SU, 2 * SU), F32)
    for p in range(16):
        tab = tabs.at[p // 2, p % 2]
        part = jnp.dot(
            planes[p].astype(BF16), turn(tab[2], tab[3]), preferred_element_type=F32
        ).astype(BF16)
        total = total + jnp.dot(
            jnp.concatenate([tab[0], tab[1]], axis=1),
            turn(part[:, :SU], part[:, SU:]),
            preferred_element_type=F32,
        )
    raw[...] = total
    keep_ref[...] = raw[pl.ds(pl.multiple_of(c * 64, 64), 64), :]
    give_ref[...] = raw[pl.ds(pl.multiple_of((1 - c) * 64, 64), 64), :]


def body(
    visibilities, coords, plane_index, block_group, offsets, facet_centre, tables, antenna_gain
):
    held = visibilities.shape[0]
    norm = SU / math.sqrt(visibilities.shape[3] * held * 8 * CH)
    named = (plane_index + 1).astype(BF16)[:, None, None]
    pack = jnp.concatenate(
        [
            visibilities.transpose(0, 2, 1, 3).reshape(held, 8, SU),
            coords,
            jnp.broadcast_to(named, (held, 1, SU)),
            jnp.zeros((held, 5, SU), BF16),
        ],
        axis=1,
    )
    table = jnp.concatenate(
        [tables[0, 0].transpose(1, 2, 0), tables[0, 1].transpose(1, 0, 2)], axis=0
    )
    vmem = pl.BlockSpec(memory_space=pltpu.VMEM)
    smem = pl.BlockSpec(memory_space=pltpu.SMEM)
    hbm = pl.BlockSpec(memory_space=pl.ANY)
    dma = pltpu.SemaphoreType.DMA
    blocks, tabs = pl.pallas_call(
        route_kernel,
        out_shape=(
            jax.ShapeDtypeStruct((8, TILES, 16, SU), BF16),
            jax.ShapeDtypeStruct((8, 2, 4, SU, SU), BF16),
        ),
        in_specs=[vmem, smem, hbm],
        out_specs=(hbm, hbm),
        scratch_shapes=[
            pltpu.VMEM((8, 2, 16, SU), BF16),
            pltpu.VMEM((8, 2, 16, SU), BF16),
            pltpu.VMEM((TILES, 16, SU), BF16),
            dma((8,)), dma((8,)), dma((8,)), dma((8,)), dma((2, 8)), dma((2, 8)), dma((2,)),
        ],
        compiler_params=pltpu.CompilerParams(
            collective_id=0, has_side_effects=True, vmem_limit_bytes=16 * 2**20
        ),
        name="route",
    )(pack, block_group, table)
    half = jax.ShapeDtypeStruct((64, 2 * SU), F32)
    keep, give = pl.pallas_call(
        grid_kernel,
        out_shape=(half, half),
        in_specs=[vmem, smem, smem, hbm],
        out_specs=(vmem, vmem),
        scratch_shapes=[
            pltpu.VMEM((128, 8, SU), F32),
            pltpu.VMEM((128, SU), F32),
            pltpu.VMEM((128, SU), F32),
            pltpu.VMEM((8, SU), jnp.int32),
            pltpu.SMEM((8, SU), jnp.int32),
            pltpu.VMEM((128, 8, SU), F32),
            pltpu.VMEM((128, 8, SU), F32),
            pltpu.VMEM((17, SU, 2 * SU), F32),
            pltpu.VMEM((8, 2, 4, SU, SU), BF16),
            pltpu.VMEM((SU, 2 * SU), F32),
            dma((2,)),
        ],
        compiler_params=pltpu.CompilerParams(vmem_limit_bytes=32 * 2**20),
        name="grid",
    )(blocks, offsets, facet_centre, tabs)
    came = lax.ppermute(give, "chan", [(0, 1), (1, 0)])
    gain_u = lax.dynamic_slice_in_dim(antenna_gain[0, 0], lax.axis_index("chan") * 64, 64)
    gains = gain_u[:, None, None] * antenna_gain[0, 1][None, None, :] * norm
    result = (keep + came).reshape(64, 2, SU) * gains
    return result.reshape(1, 1, 64, 2, SU)


def solution(mesh):
    in_specs = (
        P(("facet", "bl"), "chan", None, None),
        P(("facet", "bl"), None, None),
        P(("facet", "bl")),
        P(("facet", "bl"), None),
        P(),
        P(),
        P(("facet", "bl"), None, None, None, None),
        P("bl", None, None),
    )
    out_specs = P("facet", "bl", "chan", None, None)
    return jax.shard_map(body, mesh=mesh, in_specs=in_specs, out_specs=out_specs, check_vma=False)
```

```python
import math

import jax
import jax.numpy as jnp
from jax import lax
from jax.experimental import pallas as pl
from jax.experimental.pallas import tpu as pltpu
from jax.sharding import PartitionSpec as P

SU = 128
CH = 8
SPREAD = 1.5
ROOT = math.sqrt(math.log2(math.e) / (2.0 * SPREAD * SPREAD))
MESH = pl.DeviceIdType.MESH
F32 = jnp.float32
BF16 = jnp.bfloat16
TILES = 11
STEP = 4


def route_kernel(
    vis_ref, coord_ref, plane_hbm, group_hbm, raw_ref, blocks_ref, tabs_ref,
    plane_s, group_s, send, recv, stage, tab, a_send, a_recv, t_send, t_recv, v_send, v_recv, own_sem,
):
    f = lax.axis_index("facet")
    g = lax.axis_index("bl")
    c = lax.axis_index("chan")
    side = (f // 4) * 4
    y = lax.rem(f, 4)
    low = side + lax.rem(y + 3, 4)
    high = side + lax.rem(y + 1, 4)
    far = side + lax.rem(y + 2, 4)

    def flip(facet):
        return lax.rem(facet + 4, 8)

    up, down = (high, g, c), (low, g, c)
    beside, across = (flip(f), g, c), (flip(f), g, 1 - c)
    following = (f, lax.rem(g + 1, 8), c)

    barrier = pltpu.get_barrier_semaphore()
    for d in range(1, 8):
        for peer in ((f, lax.rem(g + d, 8), c), (lax.rem(f + d, 8), g, c)):
            pl.semaphore_signal(barrier, inc=1, device_id=peer, device_id_type=MESH)
    pl.semaphore_signal(barrier, inc=1, device_id=across, device_id_type=MESH)

    names = [
        pltpu.make_async_copy(plane_hbm, plane_s, own_sem.at[0]),
        pltpu.make_async_copy(group_hbm, group_s, own_sem.at[1]),
    ]
    for copy in names:
        copy.start()

    wide = (2 * SU, 2 * SU)
    to = lax.broadcasted_iota(jnp.int32, wide, 0)
    source = jnp.where(to < SU, 2 * to, 2 * to - (2 * SU - 1))
    pick = (source == lax.broadcasted_iota(jnp.int32, wide, 1)).astype(F32).astype(BF16)
    first = lax.dot_general(
        raw_ref[0], pick, (((0,), (1,)), ((), ())), preferred_element_type=F32
    ).astype(BF16)
    second = jnp.dot(pick, raw_ref[1], preferred_element_type=F32).astype(BF16)
    tab[0], tab[1] = first[:, :SU], first[:, SU:]
    tab[2], tab[3] = second[:SU], second[SU:]

    for copy in names:
        copy.wait()
    labels = [group_s[n, 0] for n in range(8)]
    rows = lax.broadcasted_iota(jnp.int32, (16, SU), 0)

    def build(group, carry):
        zero = jnp.int32(0)
        i0, i1, n0, n1 = zero, zero, zero, zero
        for n in reversed(range(8)):
            match = labels[n] == group
            i1 = jnp.where(match, i0, i1)
            n1 = jnp.where(match, n0, n1)
            i0 = jnp.where(match, n, i0)
            n0 = jnp.where(match, 1, n0)
        one = vis_ref[i0].astype(F32) * n0.astype(F32)
        two = vis_ref[i1].astype(F32) * n1.astype(F32)
        send[group, 0] = jnp.concatenate([one, two], axis=0).astype(BF16)
        misc = jnp.zeros((16, SU), F32)
        for k, at, here in ((0, i0, n0), (1, i1, n1)):
            spot = coord_ref[at].astype(F32)
            misc = jnp.where(rows == 3 * k, spot[0:1], misc)
            misc = jnp.where(rows == 3 * k + 1, spot[1:2], misc)
            misc = jnp.where(rows == 3 * k + 2, ((plane_s[at] + 1) * here).astype(F32), misc)
        send[group, 1] = misc.astype(BF16)
        return carry

    lax.fori_loop(0, 8, build, 0)
    pl.semaphore_wait(barrier, 15)

    def remote(sems, k, src, dst, peer):
        return pltpu.make_async_remote_copy(
            src_ref=src, dst_ref=dst, send_sem=sems[0].at[k], recv_sem=sems[1].at[k],
            device_id=peer, device_id_type=MESH,
        )

    started = []

    def go(sems, k, src, dst, peer):
        copy = remote(sems, k, src, dst, peer)
        copy.start()
        started.append(copy)

    def landed(sems, k, where):
        remote(sems, k, where, where, up).wait_recv()

    tables, visits = (t_send, t_recv), (v_send, v_recv)

    def column(facet, shift=0, half=None):
        whole = tabs_ref.at[facet, shift]
        return whole if half is None else whole.at[pl.ds(2 * half, 2)]

    def block(facet, half=None):
        whole = blocks_ref.at[facet]
        return whole if half is None else whole.at[pl.ds(6 * half, 6 - half)]

    def t_go(k, facet, peer, half=None):
        go(tables, k, column(facet, 0, half), column(facet, 0, half), peer)

    def t_shift(k, facet):
        go(tables, k, column(facet), column(facet, 1), following)

    def t_landed(k, facet, half=None):
        landed(tables, k, column(facet, 0, half))

    def v_go(k, facet, peer, half=None):
        go(visits, k, block(facet, half), block(facet, half), peer)

    def v_landed(k, facet, half=None):
        landed(visits, k, block(facet, half))

    for d in range(1, 8):
        peer = lax.rem(g + d, 8)
        copy = pltpu.make_async_remote_copy(
            src_ref=send.at[peer], dst_ref=recv.at[g], send_sem=a_send.at[d],
            recv_sem=a_recv.at[g], device_id=(f, peer, c), device_id_type=MESH,
        )
        copy.start()
        started.append(copy)
    go(tables, 0, tab, column(f), up)
    go(tables, 1, tab, column(f), down)
    go(tables, 2, tab.at[pl.ds(0, 2)], column(f, 0, 0), beside)
    go(tables, 3, tab.at[pl.ds(2, 2)], column(f, 0, 1), across)
    go(tables, 4, tab, column(f, 1), following)
    own_tab = pltpu.make_async_copy(tab, column(f), own_sem.at[0])
    own_tab.start()
    recv[g] = send[g]
    for d in range(1, 8):
        peer = lax.rem(g + d, 8)
        pltpu.make_async_remote_copy(
            src_ref=send.at[peer], dst_ref=recv.at[peer], send_sem=a_send.at[d],
            recv_sem=a_recv.at[peer], device_id=(f, peer, c), device_id_type=MESH,
        ).wait_recv()

    extra = [jnp.zeros((16, SU), F32) for _ in range(3)]
    for b in range(8):
        stage[b] = recv[b, 0]
        misc = recv[b, 1].astype(F32)
        for k in range(2):
            here = rows == 2 * b + k
            for e in range(3):
                line = 3 * k + e
                extra[e] = jnp.where(here, misc[line : line + 1], extra[e])
    for e in range(3):
        stage[8 + e] = extra[e].astype(BF16)
    go(visits, 0, stage, block(f), beside)
    go(visits, 1, stage, block(f), up)
    go(visits, 2, stage, block(f), down)
    own_blocks = pltpu.make_async_copy(stage, block(f), own_sem.at[1])
    own_blocks.start()

    t_landed(0, low)
    t_go(5, low, up, 0)
    t_go(6, low, beside, 0)
    t_go(7, low, across, 1)
    t_shift(8, low)
    t_landed(1, high)
    t_go(9, high, down, 1)
    t_go(10, high, beside, 0)
    t_go(11, high, across, 1)
    t_shift(12, high)
    v_landed(0, flip(f))
    v_go(5, flip(f), up)
    v_go(6, flip(f), down)
    v_landed(1, low)
    v_go(3, low, up, 0)
    v_landed(2, high)
    v_go(4, high, down, 1)
    t_landed(2, flip(f), 0)
    t_landed(3, flip(f), 1)
    t_shift(16, flip(f))
    v_landed(5, flip(low))
    v_go(7, flip(low), up, 0)
    v_landed(6, flip(high))
    v_go(8, flip(high), down, 1)
    t_landed(5, far, 0)
    t_go(13, far, beside, 0)
    t_landed(9, far, 1)
    t_go(14, far, across, 1)
    t_shift(15, far)
    t_landed(6, flip(low), 0)
    t_landed(7, flip(low), 1)
    t_shift(17, flip(low))
    t_landed(10, flip(high), 0)
    t_landed(11, flip(high), 1)
    t_shift(18, flip(high))
    t_landed(13, flip(far), 0)
    t_landed(14, flip(far), 1)
    t_shift(19, flip(far))
    v_landed(3, far, 0)
    v_landed(4, far, 1)
    v_landed(7, flip(far), 0)
    v_landed(8, flip(far), 1)
    for k, facet in ((4, f), (8, low), (12, high), (15, far)):
        landed(tables, k, column(facet, 1))
    for k, facet in ((16, f), (17, low), (18, high), (19, far)):
        landed(tables, k, column(flip(facet), 1))
    own_tab.wait()
    own_blocks.wait()
    for copy in started:
        copy.wait_send()


def sine_of_turns(turns):
    part = turns - jnp.floor(turns + 0.5)
    part = jnp.maximum(jnp.minimum(part, 0.5 - part), -0.5 - part)
    angle = part * (2.0 * math.pi)
    square = angle * angle
    total = jnp.full_like(angle, -1.0 / math.factorial(11))
    for power in (9, 7, 5, 3, 1):
        sign = 1.0 if power % 4 == 1 else -1.0
        total = total * square + sign / math.factorial(power)
    return total * angle


def grid_kernel(
    blocks_ref, offsets_hbm, centre_hbm, tabs_hbm, keep_ref, give_ref,
    offsets_ref, centre_ref, vis, line_u, line_v, order_v, order, turned, spots, planes, tabs, raw, sems,
):
    f = lax.axis_index("facet")
    g = lax.axis_index("bl")
    c = lax.axis_index("chan")
    fetch = pltpu.make_async_copy(tabs_hbm, tabs, sems.at[0])
    fetch.start()
    names = [
        pltpu.make_async_copy(offsets_hbm, offsets_ref, sems.at[2]),
        pltpu.make_async_copy(centre_hbm, centre_ref, sems.at[3]),
    ]
    for copy in names:
        copy.start()

    sub = lax.broadcasted_iota(jnp.int32, (SU, SU), 0)
    lane = lax.broadcasted_iota(jnp.int32, (SU, SU), 1)
    label = jnp.concatenate([blocks_ref[i, 10] for i in range(8)], axis=0)
    label = label.astype(F32).astype(jnp.int32) - 1
    number = (label >> 3) * 2 + jnp.where((label & 7) == g, 0, 1)
    number = jnp.where(label >= 0, number, 16).astype(F32)
    across = number.T
    ahead = (across < number) | ((across == number) & (lane < sub))
    place = jnp.sum(jnp.where(ahead, 1.0, 0.0), axis=1, keepdims=True)
    hit = place == lane.astype(F32)
    lines = [
        jnp.sum(jnp.where(hit, sub.astype(F32), 0.0), axis=0, keepdims=True),
        jnp.sum(jnp.where(hit, number, 0.0), axis=0, keepdims=True),
        jnp.sum(jnp.where(number < 16.0, 1.0, 0.0), axis=0, keepdims=True),
        jnp.zeros((5, SU), F32),
    ]
    order_v[...] = jnp.concatenate(lines, axis=0).astype(jnp.int32)
    orders = pltpu.make_async_copy(order_v, order, sems.at[1])
    orders.start()

    for i in range(8):
        line_u[16 * i : 16 * i + 16] = blocks_ref[i, 8].astype(F32)
        line_v[16 * i : 16 * i + 16] = blocks_ref[i, 9].astype(F32)
        for b in range(8):
            both = blocks_ref[i, b].astype(F32)
            vis[16 * i + 2 * b] = both[:8]
            vis[16 * i + 2 * b + 1] = both[8:]
    planes[...] = jnp.zeros_like(planes)
    orders.wait()
    for copy in names:
        copy.wait()
    steps = (order[2, 0] + STEP - 1) // STEP

    off_u = offsets_ref[f, g, 0].astype(F32)
    off_v = offsets_ref[f, g, 1].astype(F32)
    dir_l = centre_ref[f, 0]
    dir_m = centre_ref[f, 1]
    row = lax.broadcasted_iota(jnp.int32, (8, SU), 0)
    even = (row & 1) == 0
    channel = (c * 4 + (row >> 1)).astype(F32)
    scale = 1.0 + 0.01 * (channel - 0.5 * (CH - 1))

    def swap(pair):
        return jnp.where(even, pltpu.roll(pair, 7, 0), pltpu.roll(pair, 1, 0))

    def prepare(step, carry):
        for q in range(STEP):
            at = step * STEP + q
            slot = order[0, at]
            u = line_u[pl.ds(slot, 1), :]
            v = line_v[pl.ds(slot, 1), :]
            along = jnp.where(even, scale * u - off_u, scale * v - off_v)
            spots[at] = along * ROOT
            turns = (scale * (u * dir_l + v * dir_m)) * (1.0 / SU)
            turns = turns - jnp.floor(turns + 0.5)
            wave = sine_of_turns(turns + jnp.where(even, 0.25, 0.0))
            data = vis[slot]
            straight = data * wave
            crossed = data * swap(wave)
            turned[at] = jnp.where(even, straight - swap(straight), crossed + swap(crossed))
        return carry

    lax.fori_loop(0, steps, prepare, 0)

    cells = sub.astype(F32) * ROOT

    def profile(line):
        apart = line - cells
        return jnp.exp2(-(apart * apart)).astype(BF16)

    def gather(step, carry):
        for q in range(STEP):
            at = step * STEP + q
            along_u, real, imag = [], [], []
            for ch in range(4):
                along_u.append(profile(spots[at, 2 * ch : 2 * ch + 1, :]))
                along_v = profile(spots[at, 2 * ch + 1 : 2 * ch + 2, :])
                real.append(along_v * turned[at, 2 * ch : 2 * ch + 1, :].astype(BF16))
                imag.append(along_v * turned[at, 2 * ch + 1 : 2 * ch + 2, :].astype(BF16))
            left = jnp.concatenate(along_u, axis=1)
            right = jnp.concatenate(
                [jnp.concatenate(real, axis=1), jnp.concatenate(imag, axis=1)], axis=0
            )
            planes[order[1, at]] += lax.dot_general(
                left, right, (((1,), (1,)), ((), ())), preferred_element_type=F32
            )
        return carry

    lax.fori_loop(0, steps, gather, 0)
    fetch.wait()

    def turn(re, im):
        return jnp.concatenate(
            [jnp.concatenate([re, im], axis=1), jnp.concatenate([-im, re], axis=1)], axis=0
        )

    total = jnp.zeros((SU, 2 * SU), F32)
    for p in range(16):
        tab = tabs.at[p // 2, p % 2]
        part = jnp.dot(
            planes[p].astype(BF16), turn(tab[2], tab[3]), preferred_element_type=F32
        ).astype(BF16)
        total = total + jnp.dot(
            jnp.concatenate([tab[0], tab[1]], axis=1),
            turn(part[:, :SU], part[:, SU:]),
            preferred_element_type=F32,
        )
    raw[...] = total
    keep_ref[...] = raw[pl.ds(pl.multiple_of(c * 64, 64), 64), :]
    give_ref[...] = raw[pl.ds(pl.multiple_of((1 - c) * 64, 64), 64), :]


def body(
    visibilities, coords, plane_index, block_group, offsets, facet_centre, tables, antenna_gain
):
    held = visibilities.shape[0]
    norm = SU / math.sqrt(visibilities.shape[3] * held * 8 * CH)
    vmem = pl.BlockSpec(memory_space=pltpu.VMEM)
    hbm = pl.BlockSpec(memory_space=pl.ANY)
    dma = pltpu.SemaphoreType.DMA
    blocks, tabs = pl.pallas_call(
        route_kernel,
        out_shape=(
            jax.ShapeDtypeStruct((8, TILES, 16, SU), BF16),
            jax.ShapeDtypeStruct((8, 2, 4, SU, SU), BF16),
        ),
        in_specs=[vmem, vmem, hbm, hbm, vmem],
        out_specs=(hbm, hbm),
        scratch_shapes=[
            pltpu.SMEM((held,), jnp.int32),
            pltpu.SMEM((held, 1), jnp.int32),
            pltpu.VMEM((8, 2, 16, SU), BF16),
            pltpu.VMEM((8, 2, 16, SU), BF16),
            pltpu.VMEM((TILES, 16, SU), BF16),
            pltpu.VMEM((4, SU, SU), BF16),
            dma((8,)), dma((8,)), dma((20,)), dma((20,)), dma((9,)), dma((9,)), dma((2,)),
        ],
        compiler_params=pltpu.CompilerParams(
            collective_id=0, has_side_effects=True, vmem_limit_bytes=16 * 2**20
        ),
        name="route",
    )(
        visibilities.reshape(held, 8, SU), coords, plane_index, block_group,
        tables.reshape(2, 2 * SU, SU),
    )
    half = jax.ShapeDtypeStruct((64, 2 * SU), F32)
    keep, give = pl.pallas_call(
        grid_kernel,
        out_shape=(half, half),
        in_specs=[vmem, hbm, hbm, hbm],
        out_specs=(vmem, vmem),
        scratch_shapes=[
            pltpu.SMEM((8, 8, 2), jnp.int32),
            pltpu.SMEM((8, 2), F32),
            pltpu.VMEM((128, 8, SU), F32),
            pltpu.VMEM((128, SU), F32),
            pltpu.VMEM((128, SU), F32),
            pltpu.VMEM((8, SU), jnp.int32),
            pltpu.SMEM((8, SU), jnp.int32),
            pltpu.VMEM((128, 8, SU), F32),
            pltpu.VMEM((128, 8, SU), F32),
            pltpu.VMEM((17, SU, 2 * SU), F32),
            pltpu.VMEM((8, 2, 4, SU, SU), BF16),
            pltpu.VMEM((SU, 2 * SU), F32),
            dma((4,)),
        ],
        compiler_params=pltpu.CompilerParams(vmem_limit_bytes=32 * 2**20),
        name="grid",
    )(blocks, offsets, facet_centre, tabs)
    came = lax.ppermute(give, "chan", [(0, 1), (1, 0)])
    gain_u = lax.dynamic_slice_in_dim(antenna_gain[0, 0], lax.axis_index("chan") * 64, 64)
    gains = gain_u[:, None, None] * antenna_gain[0, 1][None, None, :] * norm
    result = (keep + came).reshape(64, 2, SU) * gains
    return result.reshape(1, 1, 64, 2, SU)


def solution(mesh):
    in_specs = (
        P(("facet", "bl"), "chan", None, None),
        P(("facet", "bl"), None, None),
        P(("facet", "bl")),
        P(("facet", "bl"), None),
        P(),
        P(),
        P(("facet", "bl"), None, None, None, None),
        P("bl", None, None),
    )
    out_specs = P("facet", "bl", "chan", None, None)
    return jax.shard_map(body, mesh=mesh, in_specs=in_specs, out_specs=out_specs, check_vma=False)
```

```python
import math

import jax
import jax.numpy as jnp
from jax import lax
from jax.experimental import pallas as pl
from jax.experimental.pallas import tpu as pltpu
from jax.sharding import PartitionSpec as P

SU = 128
CH = 8
NORM = SU / math.sqrt(128 * 8 * 8 * CH)
SPREAD = 1.5
ROOT = math.sqrt(math.log2(math.e) / (2.0 * SPREAD * SPREAD))
MESH = pl.DeviceIdType.MESH
F32 = jnp.float32
BF16 = jnp.bfloat16
TILES = 11
STEP = 8


def route_kernel(
    vis_hbm, coord_hbm, plane_hbm, group_hbm, raw_hbm, blocks_ref, tabs_ref,
    vis_ref, coord_ref, plane_s, group_s, raw_ref, send, recv, stage, tab, a_send, a_recv, t_send, t_recv, v_send, v_recv, own_sem,
):
    f = lax.axis_index("facet")
    g = lax.axis_index("bl")
    c = lax.axis_index("chan")
    side = (f // 4) * 4
    y = lax.rem(f, 4)
    low = side + lax.rem(y + 3, 4)
    high = side + lax.rem(y + 1, 4)
    far = side + lax.rem(y + 2, 4)

    def flip(facet):
        return lax.rem(facet + 4, 8)

    up, down = (high, g, c), (low, g, c)
    beside, across = (flip(f), g, c), (flip(f), g, 1 - c)

    barrier = pltpu.get_barrier_semaphore()
    for d in range(1, 8):
        for peer in ((f, lax.rem(g + d, 8), c), (lax.rem(f + d, 8), g, c)):
            pl.semaphore_signal(barrier, inc=1, device_id=peer, device_id_type=MESH)
    pl.semaphore_signal(barrier, inc=1, device_id=across, device_id_type=MESH)

    fetch_raw = pltpu.make_async_copy(raw_hbm, raw_ref, own_sem.at[2])
    fetch_raw.start()
    names = [
        pltpu.make_async_copy(group_hbm, group_s, own_sem.at[1]),
        pltpu.make_async_copy(plane_hbm, plane_s, own_sem.at[0]),
        pltpu.make_async_copy(vis_hbm, vis_ref, own_sem.at[3]),
        pltpu.make_async_copy(coord_hbm, coord_ref, own_sem.at[4]),
    ]
    for copy in names:
        copy.start()

    wide = (2 * SU, 2 * SU)
    to = lax.broadcasted_iota(jnp.int32, wide, 0)
    source = jnp.where(to < SU, 2 * to, 2 * to - (2 * SU - 1))
    pick = (source == lax.broadcasted_iota(jnp.int32, wide, 1)).astype(F32).astype(BF16)
    fetch_raw.wait()
    first = lax.dot_general(
        raw_ref[0], pick, (((0,), (1,)), ((), ())), preferred_element_type=F32
    ).astype(BF16)
    second = jnp.dot(pick, raw_ref[1], preferred_element_type=F32).astype(BF16)
    tab[0], tab[1] = first[:, :SU], first[:, SU:]
    tab[2], tab[3] = second[:SU], second[SU:]

    for copy in names:
        copy.wait()
    labels = [group_s[n] for n in range(8)]
    rows = lax.broadcasted_iota(jnp.int32, (16, SU), 0)

    def build(group, carry):
        zero = jnp.int32(0)
        i0, i1, n0, n1 = zero, zero, zero, zero
        for n in reversed(range(8)):
            match = labels[n] == group
            i1 = jnp.where(match, i0, i1)
            n1 = jnp.where(match, n0, n1)
            i0 = jnp.where(match, n, i0)
            n0 = jnp.where(match, 1, n0)
        one = vis_ref[i0].astype(F32) * n0.astype(F32)
        two = vis_ref[i1].astype(F32) * n1.astype(F32)
        send[group, 0] = jnp.concatenate([one, two], axis=0).astype(BF16)
        misc = jnp.zeros((16, SU), F32)
        for k, at, here in ((0, i0, n0), (1, i1, n1)):
            spot = coord_ref[at].astype(F32)
            misc = jnp.where(rows == 3 * k, spot[0:1], misc)
            misc = jnp.where(rows == 3 * k + 1, spot[1:2], misc)
            misc = jnp.where(rows == 3 * k + 2, ((plane_s[at] + 1) * here).astype(F32), misc)
        send[group, 1] = misc.astype(BF16)
        return carry

    lax.fori_loop(0, 8, build, 0)
    pl.semaphore_wait(barrier, 15)

    def remote(sems, k, src, dst, peer):
        return pltpu.make_async_remote_copy(
            src_ref=src, dst_ref=dst, send_sem=sems[0].at[k], recv_sem=sems[1].at[k],
            device_id=peer, device_id_type=MESH,
        )

    started = []

    def go(sems, k, src, dst, peer):
        copy = remote(sems, k, src, dst, peer)
        copy.start()
        started.append(copy)

    def landed(sems, k, where):
        remote(sems, k, where, where, up).wait_recv()

    tables, visits = (t_send, t_recv), (v_send, v_recv)

    def column(facet, half=None):
        whole = tabs_ref.at[facet]
        return whole if half is None else whole.at[pl.ds(2 * half, 2)]

    def block(facet, half=None):
        whole = blocks_ref.at[facet]
        return whole if half is None else whole.at[pl.ds(6 * half, 6 - half)]

    def t_go(k, facet, peer, half=None):
        go(tables, k, column(facet, half), column(facet, half), peer)

    def t_landed(k, facet, half=None):
        landed(tables, k, column(facet, half))

    def v_go(k, facet, peer, half=None):
        go(visits, k, block(facet, half), block(facet, half), peer)

    def v_landed(k, facet, half=None):
        landed(visits, k, block(facet, half))

    for d in range(1, 8):
        peer = lax.rem(g + d, 8)
        copy = pltpu.make_async_remote_copy(
            src_ref=send.at[peer], dst_ref=recv.at[g], send_sem=a_send.at[d],
            recv_sem=a_recv.at[g], device_id=(f, peer, c), device_id_type=MESH,
        )
        copy.start()
        started.append(copy)
    go(tables, 0, tab, column(f), up)
    go(tables, 1, tab, column(f), down)
    go(tables, 2, tab.at[pl.ds(0, 2)], column(f, 0), beside)
    go(tables, 3, tab.at[pl.ds(2, 2)], column(f, 1), across)
    own_tab = pltpu.make_async_copy(tab, column(f), own_sem.at[0])
    own_tab.start()
    recv[g] = send[g]
    for d in range(1, 8):
        peer = lax.rem(g + d, 8)
        pltpu.make_async_remote_copy(
            src_ref=send.at[peer], dst_ref=recv.at[peer], send_sem=a_send.at[d],
            recv_sem=a_recv.at[peer], device_id=(f, peer, c), device_id_type=MESH,
        ).wait_recv()

    extra = [jnp.zeros((16, SU), F32) for _ in range(3)]
    for b in range(8):
        stage[b] = recv[b, 0]
        misc = recv[b, 1].astype(F32)
        for k in range(2):
            here = rows == 2 * b + k
            for e in range(3):
                line = 3 * k + e
                extra[e] = jnp.where(here, misc[line : line + 1], extra[e])
    for e in range(3):
        stage[8 + e] = extra[e].astype(BF16)
    go(visits, 0, stage, block(f), beside)
    go(visits, 1, stage, block(f), up)
    go(visits, 2, stage, block(f), down)
    own_blocks = pltpu.make_async_copy(stage, block(f), own_sem.at[1])
    own_blocks.start()

    t_landed(0, low)
    t_go(4, low, up, 0)
    t_go(5, low, beside, 0)
    t_go(6, low, across, 1)
    t_landed(1, high)
    t_go(7, high, down, 1)
    t_go(8, high, beside, 0)
    t_go(9, high, across, 1)
    v_landed(0, flip(f))
    v_go(5, flip(f), up)
    v_go(6, flip(f), down)
    v_landed(1, low)
    v_go(3, low, up, 0)
    v_landed(2, high)
    v_go(4, high, down, 1)
    t_landed(2, flip(f), 0)
    t_landed(3, flip(f), 1)
    v_landed(5, flip(low))
    v_go(7, flip(low), up, 0)
    v_landed(6, flip(high))
    v_go(8, flip(high), down, 1)
    t_landed(4, far, 0)
    t_go(10, far, beside, 0)
    t_landed(7, far, 1)
    t_go(11, far, across, 1)
    t_landed(5, flip(low), 0)
    t_landed(6, flip(low), 1)
    t_landed(8, flip(high), 0)
    t_landed(9, flip(high), 1)
    t_landed(10, flip(far), 0)
    t_landed(11, flip(far), 1)
    v_landed(3, far, 0)
    v_landed(4, far, 1)
    v_landed(7, flip(far), 0)
    v_landed(8, flip(far), 1)
    own_tab.wait()
    own_blocks.wait()
    for copy in started:
        copy.wait_send()


def sine_of_turns(turns):
    part = turns - jnp.floor(turns + 0.5)
    part = jnp.maximum(jnp.minimum(part, 0.5 - part), -0.5 - part)
    angle = part * (2.0 * math.pi)
    square = angle * angle
    total = jnp.full_like(angle, -1.0 / math.factorial(11))
    for power in (9, 7, 5, 3, 1):
        sign = 1.0 if power % 4 == 1 else -1.0
        total = total * square + sign / math.factorial(power)
    return total * angle


def grid_kernel(
    blocks_ref, offsets_hbm, centre_hbm, sums_ref,
    offsets_ref, centre_ref, vis, line_u, line_v, order_v, order, turned, spots, planes, sems,
):
    f = lax.axis_index("facet")
    g = lax.axis_index("bl")
    c = lax.axis_index("chan")
    names = [
        pltpu.make_async_copy(offsets_hbm, offsets_ref, sems.at[0]),
        pltpu.make_async_copy(centre_hbm, centre_ref, sems.at[2]),
    ]
    for copy in names:
        copy.start()

    sub = lax.broadcasted_iota(jnp.int32, (SU, SU), 0)
    lane = lax.broadcasted_iota(jnp.int32, (SU, SU), 1)
    label = jnp.concatenate([blocks_ref[i, 10] for i in range(8)], axis=0)
    label = label.astype(F32).astype(jnp.int32) - 1
    number = (label >> 3) * 2 + jnp.where((label & 7) == g, 0, 1)
    number = jnp.where(label >= 0, number, 16).astype(F32)
    across = number.T
    ahead = (across < number) | ((across == number) & (lane < sub))
    place = jnp.sum(jnp.where(ahead, 1.0, 0.0), axis=1, keepdims=True)
    hit = place == lane.astype(F32)
    lines = [
        jnp.sum(jnp.where(hit, sub.astype(F32), 0.0), axis=0, keepdims=True),
        jnp.sum(jnp.where(hit, number, 0.0), axis=0, keepdims=True),
        jnp.sum(jnp.where(number < 16.0, 1.0, 0.0), axis=0, keepdims=True),
        jnp.zeros((5, SU), F32),
    ]
    order_v[...] = jnp.concatenate(lines, axis=0).astype(jnp.int32)
    orders = pltpu.make_async_copy(order_v, order, sems.at[1])
    orders.start()

    for i in range(8):
        line_u[16 * i : 16 * i + 16] = blocks_ref[i, 8].astype(F32)
        line_v[16 * i : 16 * i + 16] = blocks_ref[i, 9].astype(F32)
        for b in range(8):
            both = blocks_ref[i, b].astype(F32)
            vis[16 * i + 2 * b] = both[:8]
            vis[16 * i + 2 * b + 1] = both[8:]
    planes[...] = jnp.zeros_like(planes)
    orders.wait()
    for copy in names:
        copy.wait()
    steps = (order[2, 0] + STEP - 1) // STEP

    off_u = offsets_ref[f, 0, g].astype(F32)
    off_v = offsets_ref[f, 1, g].astype(F32)
    dir_l = centre_ref[0, f]
    dir_m = centre_ref[1, f]
    row = lax.broadcasted_iota(jnp.int32, (8, SU), 0)
    even = (row & 1) == 0
    channel = (c * 4 + (row >> 1)).astype(F32)
    scale = 1.0 + 0.01 * (channel - 0.5 * (CH - 1))

    def swap(pair):
        return jnp.where(even, pltpu.roll(pair, 7, 0), pltpu.roll(pair, 1, 0))

    def prepare(step, carry):
        for q in range(STEP):
            at = step * STEP + q
            slot = order[0, at]
            u = line_u[pl.ds(slot, 1), :]
            v = line_v[pl.ds(slot, 1), :]
            along = jnp.where(even, scale * u - off_u, scale * v - off_v)
            spots[at] = along * ROOT
            turns = (scale * (u * dir_l + v * dir_m)) * (1.0 / SU)
            turns = turns - jnp.floor(turns + 0.5)
            wave = sine_of_turns(turns + jnp.where(even, 0.25, 0.0))
            data = vis[slot]
            straight = data * wave
            crossed = data * swap(wave)
            turned[at] = jnp.where(even, straight - swap(straight), crossed + swap(crossed))
        return carry

    lax.fori_loop(0, steps, prepare, 0)

    cells = sub.astype(F32) * ROOT

    def profile(line):
        apart = line - cells
        return jnp.exp2(-(apart * apart)).astype(BF16)

    def gather(step, carry):
        for q in range(STEP):
            at = step * STEP + q
            along_u, real, imag = [], [], []
            for ch in range(4):
                along_u.append(profile(spots[at, 2 * ch : 2 * ch + 1, :]))
                along_v = profile(spots[at, 2 * ch + 1 : 2 * ch + 2, :])
                for line, parts in ((2 * ch, real), (2 * ch + 1, imag)):
                    weight = jnp.broadcast_to(turned[at, line : line + 1, :], (16, SU)).astype(BF16)
                    parts.append((along_v.reshape(8, 16, SU) * weight[None]).reshape(SU, SU))
            left = jnp.concatenate(along_u, axis=1)
            right = jnp.concatenate(
                [jnp.concatenate(real, axis=1), jnp.concatenate(imag, axis=1)], axis=0
            )
            planes[order[1, at]] += lax.dot_general(
                left, right, (((1,), (1,)), ((), ())), preferred_element_type=F32
            )
        return carry

    lax.fori_loop(0, steps, gather, 0)
    for p in range(16):
        sums_ref[p] = planes[p].astype(BF16)


def finish_kernel(
    sums_ref, own_hbm, shifted, gain_hbm, out_ref, gain, own, parts, give, came, sems
):
    f = lax.axis_index("facet")
    g = lax.axis_index("bl")
    c = lax.axis_index("chan")
    partner = (f, g, 1 - c)
    barrier = pltpu.get_barrier_semaphore()
    pl.semaphore_signal(barrier, inc=1, device_id=partner, device_id_type=MESH)
    fetch = pltpu.make_async_copy(own_hbm, own, sems.at[0])
    fetch.start()
    gains = pltpu.make_async_copy(gain_hbm, gain, sems.at[3])
    gains.start()

    def turn(re, im):
        return jnp.concatenate(
            [jnp.concatenate([re, im], axis=1), jnp.concatenate([-im, re], axis=1)], axis=0
        )

    for h, held in ((1, shifted), (0, own)):
        if h == 0:
            fetch.wait()
        for i in range(8):
            part = jnp.dot(
                sums_ref[2 * i + h], turn(held[i, 2], held[i, 3]), preferred_element_type=F32
            ).astype(BF16)
            parts[8 * h + i] = turn(part[:, :SU], part[:, SU:])

    def rows_of(half):
        rows = pl.ds(pl.multiple_of(half * 64, 64), 64)
        total = jnp.zeros((64, 2 * SU), F32)
        for h, held in enumerate((own, shifted)):
            for i in range(8):
                matrix = jnp.concatenate([held[i, 0, rows], held[i, 1, rows]], axis=1)
                total = total + jnp.dot(matrix, parts[8 * h + i], preferred_element_type=F32)
        return total

    give[...] = rows_of(1 - c)
    pl.semaphore_wait(barrier, 1)
    copy = pltpu.make_async_remote_copy(
        src_ref=give, dst_ref=came, send_sem=sems.at[1], recv_sem=sems.at[2],
        device_id=partner, device_id_type=MESH,
    )
    copy.start()
    keep = rows_of(c)
    gains.wait()
    tall = (64, SU)
    mine = lax.broadcasted_iota(jnp.int32, tall, 1) == lax.broadcasted_iota(jnp.int32, tall, 0) + c * 64
    along_u = jnp.sum(jnp.where(mine, gain[0, 0:1], 0.0), axis=1, keepdims=True)
    both = along_u * gain[0, 1:2] * NORM
    copy.wait()
    out_ref[...] = (keep + came[...]) * jnp.concatenate([both, both], axis=1)


def body(
    visibilities, coords, plane_index, block_group, offsets, facet_centre, tables, antenna_gain
):
    held = visibilities.shape[0]
    vmem = pl.BlockSpec(memory_space=pltpu.VMEM)
    hbm = pl.BlockSpec(memory_space=pltpu.HBM)
    loose = pl.BlockSpec(memory_space=pl.ANY)
    dma = pltpu.SemaphoreType.DMA
    blocks, tabs = pl.pallas_call(
        route_kernel,
        out_shape=(
            jax.ShapeDtypeStruct((8, TILES, 16, SU), BF16),
            jax.ShapeDtypeStruct((8, 4, SU, SU), BF16),
        ),
        in_specs=[hbm] * 5,
        out_specs=(loose, loose),
        scratch_shapes=[
            pltpu.VMEM((held, 8, SU), BF16),
            pltpu.VMEM((held, 2, SU), BF16),
            pltpu.SMEM((held,), jnp.int32),
            pltpu.SMEM((held,), jnp.int32),
            pltpu.VMEM((2, 2 * SU, SU), BF16),
            pltpu.VMEM((8, 2, 16, SU), BF16),
            pltpu.VMEM((8, 2, 16, SU), BF16),
            pltpu.VMEM((TILES, 16, SU), BF16),
            pltpu.VMEM((4, SU, SU), BF16),
            dma((8,)), dma((8,)), dma((12,)), dma((12,)), dma((9,)), dma((9,)), dma((5,)),
        ],
        compiler_params=pltpu.CompilerParams(
            collective_id=0, has_side_effects=True, vmem_limit_bytes=60 * 2**20
        ),
        name="route",
    )(
        visibilities.reshape(held, 8, SU), coords, plane_index, block_group.reshape(held),
        tables.reshape(2, 2 * SU, SU),
    )
    shifted = lax.ppermute(tabs, "bl", [(i, (i + 1) % 8) for i in range(8)])
    sums = pl.pallas_call(
        grid_kernel,
        out_shape=jax.ShapeDtypeStruct((16, SU, 2 * SU), BF16),
        in_specs=[vmem, hbm, hbm],
        out_specs=vmem,
        scratch_shapes=[
            pltpu.SMEM((8, 2, 8), jnp.int32),
            pltpu.SMEM((2, 8), F32),
            pltpu.VMEM((128, 8, SU), F32),
            pltpu.VMEM((128, SU), F32),
            pltpu.VMEM((128, SU), F32),
            pltpu.VMEM((8, SU), jnp.int32),
            pltpu.SMEM((8, SU), jnp.int32),
            pltpu.VMEM((128, 8, SU), F32),
            pltpu.VMEM((128, 8, SU), F32),
            pltpu.VMEM((17, SU, 2 * SU), F32),
            dma((3,)),
        ],
        compiler_params=pltpu.CompilerParams(vmem_limit_bytes=40 * 2**20),
        cost_estimate=pl.CostEstimate(
            flops=5 * 10**9, bytes_accessed=2 * 10**6, transcendentals=10**7
        ),
        name="grid",
    )(blocks, offsets.transpose(0, 2, 1), facet_centre.T)
    rows_sum = pl.pallas_call(
        finish_kernel,
        out_shape=jax.ShapeDtypeStruct((64, 2 * SU), F32),
        in_specs=[vmem, hbm, vmem, hbm],
        out_specs=vmem,
        scratch_shapes=[
            pltpu.VMEM((1, 2, SU), F32),
            pltpu.VMEM((8, 4, SU, SU), BF16),
            pltpu.VMEM((16, 2 * SU, 2 * SU), BF16),
            pltpu.VMEM((64, 2 * SU), F32),
            pltpu.VMEM((64, 2 * SU), F32),
            dma((4,)),
        ],
        compiler_params=pltpu.CompilerParams(
            collective_id=1, has_side_effects=True, vmem_limit_bytes=24 * 2**20
        ),
        name="finish",
    )(sums, tabs, shifted, antenna_gain)
    return rows_sum.reshape(1, 1, 64, 2, SU)


def solution(mesh):
    in_specs = (
        P(("facet", "bl"), "chan", None, None),
        P(("facet", "bl"), None, None),
        P(("facet", "bl")),
        P(("facet", "bl"), None),
        P(),
        P(),
        P(("facet", "bl"), None, None, None, None),
        P("bl", None, None),
    )
    out_specs = P("facet", "bl", "chan", None, None)
    return jax.shard_map(body, mesh=mesh, in_specs=in_specs, out_specs=out_specs, check_vma=False)
```

```python
import math

import jax
import jax.numpy as jnp
from jax import lax
from jax.experimental import pallas as pl
from jax.experimental.pallas import tpu as pltpu
from jax.sharding import PartitionSpec as P

SU = 128
CH = 8
NORM = SU / math.sqrt(128 * 8 * 8 * CH)
SPREAD = 1.5
ROOT = math.sqrt(math.log2(math.e) / (2.0 * SPREAD * SPREAD))
MESH = pl.DeviceIdType.MESH
F32 = jnp.float32
BF16 = jnp.bfloat16
TILES = 11
STEP = 16


def route_kernel(
    vis_hbm, coord_hbm, plane_hbm, group_hbm, raw_hbm, offsets_hbm, centre_hbm, gain_hbm,
    blocks_ref, near_ref, ring_ref, shifted_ref,
    vis_ref, coord_ref, plane_s, group_s, raw_ref, offsets_s, centre_s, gain, constants,
    send, recv, stage, tab, a_send, a_recv, t_send, t_recv, v_send, v_recv, own_sem,
):
    f = lax.axis_index("facet")
    g = lax.axis_index("bl")
    c = lax.axis_index("chan")
    side = (f // 4) * 4
    y = lax.rem(f, 4)
    low = side + lax.rem(y + 3, 4)
    high = side + lax.rem(y + 1, 4)
    far = side + lax.rem(y + 2, 4)

    def flip(facet):
        return lax.rem(facet + 4, 8)

    up, down = (high, g, c), (low, g, c)
    beside, across = (flip(f), g, c), (flip(f), g, 1 - c)
    following = (f, lax.rem(g + 1, 8), c)

    barrier = pltpu.get_barrier_semaphore()
    for d in range(1, 8):
        for peer in ((f, lax.rem(g + d, 8), c), (lax.rem(f + d, 8), g, c)):
            pl.semaphore_signal(barrier, inc=1, device_id=peer, device_id_type=MESH)
    pl.semaphore_signal(barrier, inc=1, device_id=across, device_id_type=MESH)

    fetch_raw = pltpu.make_async_copy(raw_hbm, raw_ref, own_sem.at[2])
    fetch_raw.start()
    names = [
        pltpu.make_async_copy(group_hbm, group_s, own_sem.at[1]),
        pltpu.make_async_copy(plane_hbm, plane_s, own_sem.at[0]),
        pltpu.make_async_copy(vis_hbm, vis_ref, own_sem.at[3]),
        pltpu.make_async_copy(coord_hbm, coord_ref, own_sem.at[4]),
        pltpu.make_async_copy(offsets_hbm, offsets_s, own_sem.at[5]),
        pltpu.make_async_copy(centre_hbm, centre_s, own_sem.at[6]),
        pltpu.make_async_copy(gain_hbm, gain, own_sem.at[7]),
    ]
    for copy in names:
        copy.start()

    wide = (2 * SU, 2 * SU)
    to = lax.broadcasted_iota(jnp.int32, wide, 0)
    source = jnp.where(to < SU, 2 * to, 2 * to - (2 * SU - 1))
    pick = (source == lax.broadcasted_iota(jnp.int32, wide, 1)).astype(F32).astype(BF16)
    fetch_raw.wait()
    first = lax.dot_general(
        raw_ref[0], pick, (((0,), (1,)), ((), ())), preferred_element_type=F32
    ).astype(BF16)
    second = jnp.dot(pick, raw_ref[1], preferred_element_type=F32).astype(BF16)
    tab[0], tab[1] = first[:, :SU], first[:, SU:]
    tab[2], tab[3] = second[:SU], second[SU:]

    for copy in names:
        copy.wait()
    labels = [group_s[n] for n in range(8)]
    rows = lax.broadcasted_iota(jnp.int32, (16, SU), 0)

    def build(group, carry):
        zero = jnp.int32(0)
        i0, i1, n0, n1 = zero, zero, zero, zero
        for n in reversed(range(8)):
            match = labels[n] == group
            i1 = jnp.where(match, i0, i1)
            n1 = jnp.where(match, n0, n1)
            i0 = jnp.where(match, n, i0)
            n0 = jnp.where(match, 1, n0)
        one = vis_ref[i0].astype(F32) * n0.astype(F32)
        two = vis_ref[i1].astype(F32) * n1.astype(F32)
        send[group, 0] = jnp.concatenate([one, two], axis=0).astype(BF16)
        misc = jnp.zeros((16, SU), F32)
        for k, at, here in ((0, i0, n0), (1, i1, n1)):
            spot = coord_ref[at].astype(F32)
            misc = jnp.where(rows == 3 * k, spot[0:1], misc)
            misc = jnp.where(rows == 3 * k + 1, spot[1:2], misc)
            misc = jnp.where(rows == 3 * k + 2, ((plane_s[at] + 1) * here).astype(F32), misc)
        send[group, 1] = misc.astype(BF16)
        return carry

    lax.fori_loop(0, 8, build, 0)

    def line(value):
        return jnp.full((1, SU), value, F32)

    lines = [line(offsets_s[f, k, g].astype(F32)) for k in range(2)]
    for value in (line(centre_s[0, f]), line(centre_s[1, f]), gain[0, 0:1], gain[0, 1:2]):
        for _ in range(3):
            term = value.astype(BF16).astype(F32)
            lines.append(term)
            value = value - term
    lines.append(jnp.zeros((2, SU), F32))
    constants[0] = jnp.concatenate(lines, axis=0).astype(BF16)
    own_constants = pltpu.make_async_copy(constants, blocks_ref.at[pl.ds(88, 1)], own_sem.at[5])
    own_constants.start()
    pl.semaphore_wait(barrier, 15)

    def remote(sems, k, src, dst, peer):
        return pltpu.make_async_remote_copy(
            src_ref=src, dst_ref=dst, send_sem=sems[0].at[k], recv_sem=sems[1].at[k],
            device_id=peer, device_id_type=MESH,
        )

    started = []

    def go(sems, k, src, dst, peer):
        copy = remote(sems, k, src, dst, peer)
        copy.start()
        started.append(copy)

    def landed(sems, k, where):
        remote(sems, k, where, where, up).wait_recv()

    tables, visits = (t_send, t_recv), (v_send, v_recv)

    own_at, flip_at = near_ref.at[0], near_ref.at[1]

    def part(table, half):
        return table.at[pl.ds(2 * half, 2)]

    def sides(half, i):
        return part(ring_ref.at[i], half)

    def block(facet):
        return blocks_ref.at[pl.ds(facet * TILES, TILES)]

    def t_go(k, source, target, peer):
        go(tables, k, source, target, peer)

    def t_landed(k, where):
        landed(tables, k, where)

    for d in range(1, 8):
        peer = lax.rem(g + d, 8)
        copy = pltpu.make_async_remote_copy(
            src_ref=send.at[peer], dst_ref=recv.at[g], send_sem=a_send.at[d],
            recv_sem=a_recv.at[g], device_id=(f, peer, c), device_id_type=MESH,
        )
        copy.start()
        started.append(copy)
    t_go(0, part(tab, 0), sides(0, 0), up)
    t_go(1, part(tab, 1), sides(1, 1), down)
    t_go(2, part(tab, 1), sides(1, 0), up)
    t_go(3, part(tab, 0), sides(0, 1), down)
    t_go(4, part(tab, 0), part(flip_at, 0), beside)
    t_go(5, part(tab, 1), part(flip_at, 1), across)
    t_go(6, tab, shifted_ref.at[0], following)
    own_tab = pltpu.make_async_copy(tab, own_at, own_sem.at[0])
    own_tab.start()
    recv[g] = send[g]
    for d in range(1, 8):
        peer = lax.rem(g + d, 8)
        pltpu.make_async_remote_copy(
            src_ref=send.at[peer], dst_ref=recv.at[peer], send_sem=a_send.at[d],
            recv_sem=a_recv.at[peer], device_id=(f, peer, c), device_id_type=MESH,
        ).wait_recv()

    extra = [jnp.zeros((16, SU), F32) for _ in range(3)]
    for b in range(8):
        stage[b] = recv[b, 0]
        misc = recv[b, 1].astype(F32)
        for k in range(2):
            here = rows == 2 * b + k
            for e in range(3):
                line = 3 * k + e
                extra[e] = jnp.where(here, misc[line : line + 1], extra[e])
    for e in range(3):
        stage[8 + e] = extra[e].astype(BF16)
    peers = (flip(f), high, low, flip(high), flip(low), far, flip(far))
    for k, facet in enumerate(peers):
        go(visits, k, stage, block(f), (facet, g, c))
    own_blocks = pltpu.make_async_copy(stage, block(f), own_sem.at[1])
    own_blocks.start()

    t_landed(0, sides(0, 0))
    t_go(7, sides(0, 0), sides(0, 2), up)
    t_landed(1, sides(1, 1))
    t_go(8, sides(1, 1), sides(1, 2), down)
    t_landed(4, part(flip_at, 0))
    t_landed(5, part(flip_at, 1))
    t_go(9, flip_at, shifted_ref.at[1], following)
    sources = (flip(f), low, high, flip(low), flip(high), far, flip(far))
    for k, facet in enumerate(sources):
        landed(visits, k, block(facet))
    t_landed(2, sides(1, 0))
    t_landed(3, sides(0, 1))
    t_landed(6, shifted_ref.at[0])
    t_landed(7, sides(0, 2))
    t_landed(8, sides(1, 2))
    t_landed(9, shifted_ref.at[1])
    own_constants.wait()
    own_tab.wait()
    own_blocks.wait()
    for copy in started:
        copy.wait_send()


def sine_of_turns(turns):
    part = turns - jnp.floor(turns + 0.5)
    part = jnp.maximum(jnp.minimum(part, 0.5 - part), -0.5 - part)
    angle = part * (2.0 * math.pi)
    square = angle * angle
    total = jnp.full_like(angle, -1.0 / math.factorial(11))
    for power in (9, 7, 5, 3, 1):
        sign = 1.0 if power % 4 == 1 else -1.0
        total = total * square + sign / math.factorial(power)
    return total * angle


def grid_kernel(
    blocks_ref, sums_ref, gains_ref, vis, line_u, line_v, order_v, order, turned, spots, planes, sems,
):
    f = lax.axis_index("facet")
    g = lax.axis_index("bl")
    c = lax.axis_index("chan")
    sub = lax.broadcasted_iota(jnp.int32, (SU, SU), 0)
    lane = lax.broadcasted_iota(jnp.int32, (SU, SU), 1)
    label = jnp.concatenate([blocks_ref[TILES * i + 10] for i in range(8)], axis=0)
    label = label.astype(F32).astype(jnp.int32) - 1
    number = (label >> 3) * 2 + jnp.where((label & 7) == g, 0, 1)
    number = jnp.where(label >= 0, number, 16).astype(F32)
    across = number.T
    ahead = (across < number) | ((across == number) & (lane < sub))
    place = jnp.sum(jnp.where(ahead, 1.0, 0.0), axis=1, keepdims=True)
    hit = place == lane.astype(F32)
    lines = [
        jnp.sum(jnp.where(hit, sub.astype(F32), 0.0), axis=0, keepdims=True),
        jnp.sum(jnp.where(hit, number, 0.0), axis=0, keepdims=True),
        jnp.sum(jnp.where(number < 16.0, 1.0, 0.0), axis=0, keepdims=True),
        jnp.zeros((5, SU), F32),
    ]
    order_v[...] = jnp.concatenate(lines, axis=0).astype(jnp.int32)
    orders = pltpu.make_async_copy(order_v, order, sems.at[0])
    orders.start()

    for i in range(8):
        line_u[16 * i : 16 * i + 16] = blocks_ref[TILES * i + 8].astype(F32)
        line_v[16 * i : 16 * i + 16] = blocks_ref[TILES * i + 9].astype(F32)
        for b in range(8):
            both = blocks_ref[TILES * i + b].astype(F32)
            vis[16 * i + 2 * b] = both[:8]
            vis[16 * i + 2 * b + 1] = both[8:]
    planes[...] = jnp.zeros_like(planes)
    lines = blocks_ref[8 * TILES].astype(F32)
    off_u, off_v = lines[0:1], lines[1:2]
    dir_l, dir_m, gain_u, gain_v = [
        lines[k : k + 1] + lines[k + 1 : k + 2] + lines[k + 2 : k + 3] for k in (2, 5, 8, 11)
    ]
    tall = (64, SU)
    mine = lax.broadcasted_iota(jnp.int32, tall, 1) == lax.broadcasted_iota(jnp.int32, tall, 0) + c * 64
    along_j = jnp.sum(jnp.where(mine, gain_u, 0.0), axis=1, keepdims=True)
    gains_ref[...] = along_j * gain_v * NORM
    orders.wait()
    count = order[2, 0]
    wide = (count + STEP // 2 - 1) // STEP
    narrow = jnp.where(count > wide * STEP, 1, 0)

    row = lax.broadcasted_iota(jnp.int32, (8, SU), 0)
    even = (row & 1) == 0
    channel = (c * 4 + (row >> 1)).astype(F32)
    scale = 1.0 + 0.01 * (channel - 0.5 * (CH - 1))

    def swap(pair):
        return jnp.where(even, pltpu.roll(pair, 7, 0), pltpu.roll(pair, 1, 0))

    def prepare(first, size):
        for q in range(size):
            at = first + q
            slot = order[0, at]
            u = line_u[pl.ds(slot, 1), :]
            v = line_v[pl.ds(slot, 1), :]
            along = jnp.where(even, scale * u - off_u, scale * v - off_v)
            spots[at] = along * ROOT
            turns = (scale * (u * dir_l + v * dir_m)) * (1.0 / SU)
            turns = turns - jnp.floor(turns + 0.5)
            wave = sine_of_turns(turns + jnp.where(even, 0.25, 0.0))
            data = vis[slot]
            straight = data * wave
            crossed = data * swap(wave)
            turned[at] = jnp.where(even, straight - swap(straight), crossed + swap(crossed))

    def every(work):
        def one(step, carry):
            work(step * STEP, STEP)
            return carry

        def rest(step, carry):
            work(wide * STEP, STEP // 2)
            return carry

        lax.fori_loop(0, wide, one, 0)
        lax.fori_loop(0, narrow, rest, 0)

    every(prepare)

    cells = sub.astype(F32) * ROOT

    def profile(line):
        apart = line - cells
        return jnp.exp2(-(apart * apart)).astype(BF16)

    def gather(first, size):
        for q in range(size):
            at = first + q
            along_u, real, imag = [], [], []
            for ch in range(4):
                along_u.append(profile(spots[at, 2 * ch : 2 * ch + 1, :]))
                along_v = profile(spots[at, 2 * ch + 1 : 2 * ch + 2, :])
                for line, parts in ((2 * ch, real), (2 * ch + 1, imag)):
                    weight = jnp.broadcast_to(turned[at, line : line + 1, :], (16, SU)).astype(BF16)
                    parts.append((along_v.reshape(8, 16, SU) * weight[None]).reshape(SU, SU))
            left = jnp.concatenate(along_u, axis=1)
            right = jnp.concatenate(
                [jnp.concatenate(real, axis=1), jnp.concatenate(imag, axis=1)], axis=0
            )
            planes[order[1, at]] += lax.dot_general(
                left, right, (((1,), (1,)), ((), ())), preferred_element_type=F32
            )

    every(gather)
    for p in range(16):
        sums_ref[p] = planes[p].astype(BF16)


def finish_kernel(
    sums_ref, gains_ref, near, ring, shifted, beside, after, both_ways, out_ref, parts, give, came, sems,
):
    f = lax.axis_index("facet")
    g = lax.axis_index("bl")
    c = lax.axis_index("chan")
    partner = (f, g, 1 - c)
    barrier = pltpu.get_barrier_semaphore()
    pl.semaphore_signal(barrier, inc=1, device_id=partner, device_id_type=MESH)
    def turn(re, im):
        return jnp.concatenate(
            [jnp.concatenate([re, im], axis=1), jnp.concatenate([-im, re], axis=1)], axis=0
        )

    side = (f // 4) * 4
    y = lax.rem(f, 4)
    low, high, far = [side + lax.rem(y + d, 4) for d in (3, 1, 2)]

    def flip(facet):
        return lax.rem(facet + 4, 8)

    planes = []
    for shift, ends, round_y, flipped in ((0, near, ring, beside), (1, shifted, after, both_ways)):
        for facet, table in (
            (f, ends.at[0]), (flip(f), ends.at[1]),
            (low, round_y.at[0]), (high, round_y.at[1]), (far, round_y.at[2]),
            (flip(low), flipped.at[0]), (flip(high), flipped.at[1]), (flip(far), flipped.at[2]),
        ):
            planes.append((2 * facet + shift, table))
    for k, (plane, table) in enumerate(planes):
        part = jnp.dot(
            sums_ref[plane], turn(table[2], table[3]), preferred_element_type=F32
        ).astype(BF16)
        parts[k] = turn(part[:, :SU], part[:, SU:])

    def rows_of(half):
        rows = pl.ds(pl.multiple_of(half * 64, 64), 64)
        total = jnp.zeros((64, 2 * SU), F32)
        for k, (_, table) in enumerate(planes):
            both = jnp.concatenate([table[0, rows], table[1, rows]], axis=1)
            total = total + jnp.dot(both, parts[k], preferred_element_type=F32)
        return total

    give[...] = rows_of(1 - c).astype(BF16)
    pl.semaphore_wait(barrier, 1)
    copy = pltpu.make_async_remote_copy(
        src_ref=give, dst_ref=came, send_sem=sems.at[0], recv_sem=sems.at[1],
        device_id=partner, device_id_type=MESH,
    )
    copy.start()
    keep = rows_of(c)
    both = jnp.concatenate([gains_ref[...], gains_ref[...]], axis=1)
    copy.wait()
    out_ref[...] = (keep + came[...].astype(F32)) * both


def body(
    visibilities, coords, plane_index, block_group, offsets, facet_centre, tables, antenna_gain
):
    held = visibilities.shape[0]
    vmem = pl.BlockSpec(memory_space=pltpu.VMEM)
    hbm = pl.BlockSpec(memory_space=pltpu.HBM)
    loose = pl.BlockSpec(memory_space=pl.ANY)
    dma = pltpu.SemaphoreType.DMA
    pair = jax.ShapeDtypeStruct((2, 4, SU, SU), BF16)
    three = jax.ShapeDtypeStruct((3, 4, SU, SU), BF16)
    blocks, near, ring, shifted = pl.pallas_call(
        route_kernel,
        out_shape=(jax.ShapeDtypeStruct((8 * TILES + 1, 16, SU), BF16), pair, three, pair),
        in_specs=[hbm] * 8,
        out_specs=(loose,) * 4,
        scratch_shapes=[
            pltpu.VMEM((held, 8, SU), BF16),
            pltpu.VMEM((held, 2, SU), BF16),
            pltpu.SMEM((held,), jnp.int32),
            pltpu.SMEM((held,), jnp.int32),
            pltpu.VMEM((2, 2 * SU, SU), BF16),
            pltpu.SMEM((8, 2, 8), jnp.int32),
            pltpu.SMEM((2, 8), F32),
            pltpu.VMEM((1, 2, SU), F32),
            pltpu.VMEM((1, 16, SU), BF16),
            pltpu.VMEM((8, 2, 16, SU), BF16),
            pltpu.VMEM((8, 2, 16, SU), BF16),
            pltpu.VMEM((TILES, 16, SU), BF16),
            pltpu.VMEM((4, SU, SU), BF16),
            dma((8,)), dma((8,)), dma((10,)), dma((10,)), dma((7,)), dma((7,)), dma((8,)),
        ],
        compiler_params=pltpu.CompilerParams(
            collective_id=0, has_side_effects=True, vmem_limit_bytes=58 * 2**20
        ),
        name="route",
    )(
        visibilities.reshape(held, 8, SU), coords, plane_index, block_group.reshape(held),
        tables.reshape(2, 2 * SU, SU), offsets.transpose(0, 2, 1), facet_centre.T, antenna_gain,
    )
    axes = ("facet", "bl", "chan")
    devices = [(f, g, c) for f in range(8) for g in range(8) for c in range(2)]

    def number(f, g, c):
        return (f * 8 + g) * 2 + c

    def moved(array, facets, groups, chans):
        pairs = [
            (number(f, g, c), number((f + facets) % 8, (g + groups) % 8, (c + chans) % 2))
            for f, g, c in devices
        ]
        return lax.ppermute(array, axes, pairs)

    others = [moved(ring, *way) for way in ((4, 0, 0), (0, 1, 0), (4, 1, 1))]
    sums, gains = pl.pallas_call(
        grid_kernel,
        out_shape=(
            jax.ShapeDtypeStruct((16, SU, 2 * SU), BF16),
            jax.ShapeDtypeStruct((64, SU), F32),
        ),
        in_specs=[vmem],
        out_specs=(vmem, vmem),
        scratch_shapes=[
            pltpu.VMEM((128, 8, SU), F32),
            pltpu.VMEM((128, SU), F32),
            pltpu.VMEM((128, SU), F32),
            pltpu.VMEM((8, SU), jnp.int32),
            pltpu.SMEM((8, SU), jnp.int32),
            pltpu.VMEM((128, 8, SU), F32),
            pltpu.VMEM((128, 8, SU), F32),
            pltpu.VMEM((17, SU, 2 * SU), F32),
            dma((1,)),
        ],
        compiler_params=pltpu.CompilerParams(vmem_limit_bytes=40 * 2**20),
        cost_estimate=pl.CostEstimate(
            flops=5 * 10**9, bytes_accessed=2 * 10**6, transcendentals=10**7
        ),
        name="grid",
    )(blocks)
    rows_sum = pl.pallas_call(
        finish_kernel,
        out_shape=jax.ShapeDtypeStruct((64, 2 * SU), F32),
        in_specs=[vmem] * 8,
        out_specs=vmem,
        scratch_shapes=[
            pltpu.VMEM((16, 2 * SU, 2 * SU), BF16),
            pltpu.VMEM((64, 2 * SU), BF16),
            pltpu.VMEM((64, 2 * SU), BF16),
            dma((2,)),
        ],
        compiler_params=pltpu.CompilerParams(
            collective_id=1, has_side_effects=True, vmem_limit_bytes=24 * 2**20
        ),
        name="finish",
    )(sums, gains, near, ring, shifted, *others)
    return rows_sum.reshape(1, 1, 64, 2, SU)


def solution(mesh):
    in_specs = (
        P(("facet", "bl"), "chan", None, None),
        P(("facet", "bl"), None, None),
        P(("facet", "bl")),
        P(("facet", "bl"), None),
        P(),
        P(),
        P(("facet", "bl"), None, None, None, None),
        P("bl", None, None),
    )
    out_specs = P("facet", "bl", "chan", None, None)
    return jax.shard_map(body, mesh=mesh, in_specs=in_specs, out_specs=out_specs, check_vma=False)
```

```python
import math

import jax
import jax.numpy as jnp
from jax import lax
from jax.experimental import pallas as pl
from jax.experimental.pallas import tpu as pltpu
from jax.sharding import PartitionSpec as P

SU = 128
CH = 8
NORM = SU / math.sqrt(128 * 8 * 8 * CH)
SPREAD = 1.5
ROOT = math.sqrt(math.log2(math.e) / (2.0 * SPREAD * SPREAD))
MESH = pl.DeviceIdType.MESH
F32 = jnp.float32
BF16 = jnp.bfloat16
TILES = 11


def route_kernel(
    vis_hbm, coord_hbm, plane_hbm, group_hbm, raw_hbm, offsets_hbm, centre_hbm, gain_hbm,
    blocks_ref, near_ref, ring_ref, shifted_ref,
    vis_ref, coord_ref, plane_s, group_s, raw_ref, offsets_s, centre_s, gain, constants,
    send, recv, stage, tab, a_send, a_recv, t_send, t_recv, v_send, v_recv, own_sem,
):
    f = lax.axis_index("facet")
    g = lax.axis_index("bl")
    c = lax.axis_index("chan")
    side = (f // 4) * 4
    y = lax.rem(f, 4)
    low = side + lax.rem(y + 3, 4)
    high = side + lax.rem(y + 1, 4)
    far = side + lax.rem(y + 2, 4)

    def flip(facet):
        return lax.rem(facet + 4, 8)

    up, down = (high, g, c), (low, g, c)
    beside, across = (flip(f), g, c), (flip(f), g, 1 - c)
    following = (f, lax.rem(g + 1, 8), c)

    barrier = pltpu.get_barrier_semaphore()
    for d in range(1, 8):
        for peer in ((f, lax.rem(g + d, 8), c), (lax.rem(f + d, 8), g, c)):
            pl.semaphore_signal(barrier, inc=1, device_id=peer, device_id_type=MESH)
    pl.semaphore_signal(barrier, inc=1, device_id=across, device_id_type=MESH)

    fetch_raw = pltpu.make_async_copy(raw_hbm, raw_ref, own_sem.at[2])
    fetch_raw.start()
    names = [
        pltpu.make_async_copy(group_hbm, group_s, own_sem.at[1]),
        pltpu.make_async_copy(plane_hbm, plane_s, own_sem.at[0]),
        pltpu.make_async_copy(vis_hbm, vis_ref, own_sem.at[3]),
        pltpu.make_async_copy(coord_hbm, coord_ref, own_sem.at[4]),
        pltpu.make_async_copy(offsets_hbm, offsets_s, own_sem.at[5]),
        pltpu.make_async_copy(centre_hbm, centre_s, own_sem.at[6]),
        pltpu.make_async_copy(gain_hbm, gain, own_sem.at[7]),
    ]
    for copy in names:
        copy.start()

    wide = (2 * SU, 2 * SU)
    to = lax.broadcasted_iota(jnp.int32, wide, 0)
    source = jnp.where(to < SU, 2 * to, 2 * to - (2 * SU - 1))
    pick = (source == lax.broadcasted_iota(jnp.int32, wide, 1)).astype(F32).astype(BF16)
    fetch_raw.wait()
    first = lax.dot_general(
        raw_ref[0], pick, (((0,), (1,)), ((), ())), preferred_element_type=F32
    ).astype(BF16)
    second = jnp.dot(pick, raw_ref[1], preferred_element_type=F32).astype(BF16)
    tab[0], tab[1] = first[:, :SU], first[:, SU:]
    tab[2], tab[3] = second[:SU], second[SU:]

    for copy in names:
        copy.wait()
    labels = [group_s[n] for n in range(8)]
    rows = lax.broadcasted_iota(jnp.int32, (16, SU), 0)

    def build(group, carry):
        zero = jnp.int32(0)
        i0, i1, n0, n1 = zero, zero, zero, zero
        for n in reversed(range(8)):
            match = labels[n] == group
            i1 = jnp.where(match, i0, i1)
            n1 = jnp.where(match, n0, n1)
            i0 = jnp.where(match, n, i0)
            n0 = jnp.where(match, 1, n0)
        one = vis_ref[i0].astype(F32) * n0.astype(F32)
        two = vis_ref[i1].astype(F32) * n1.astype(F32)
        send[group, 0] = jnp.concatenate([one, two], axis=0).astype(BF16)
        misc = jnp.zeros((16, SU), F32)
        for k, at, here in ((0, i0, n0), (1, i1, n1)):
            spot = coord_ref[at].astype(F32)
            misc = jnp.where(rows == 3 * k, spot[0:1], misc)
            misc = jnp.where(rows == 3 * k + 1, spot[1:2], misc)
            misc = jnp.where(rows == 3 * k + 2, ((plane_s[at] + 1) * here).astype(F32), misc)
        send[group, 1] = misc.astype(BF16)
        return carry

    lax.fori_loop(0, 8, build, 0)

    def line(value):
        return jnp.full((1, SU), value, F32)

    lines = [line(offsets_s[f, k, g].astype(F32)) for k in range(2)]
    for value in (line(centre_s[0, f]), line(centre_s[1, f]), gain[0, 0:1], gain[0, 1:2]):
        for _ in range(3):
            term = value.astype(BF16).astype(F32)
            lines.append(term)
            value = value - term
    lines.append(jnp.zeros((2, SU), F32))
    constants[0] = jnp.concatenate(lines, axis=0).astype(BF16)
    own_constants = pltpu.make_async_copy(constants, blocks_ref.at[pl.ds(88, 1)], own_sem.at[5])
    own_constants.start()
    pl.semaphore_wait(barrier, 15)

    def remote(sems, k, src, dst, peer):
        return pltpu.make_async_remote_copy(
            src_ref=src, dst_ref=dst, send_sem=sems[0].at[k], recv_sem=sems[1].at[k],
            device_id=peer, device_id_type=MESH,
        )

    started = []

    def go(sems, k, src, dst, peer):
        copy = remote(sems, k, src, dst, peer)
        copy.start()
        started.append(copy)

    def landed(sems, k, where):
        remote(sems, k, where, where, up).wait_recv()

    tables, visits = (t_send, t_recv), (v_send, v_recv)

    own_at, flip_at, low_at, flip_low_at = [near_ref.at[i] for i in range(4)]

    def part(table, half):
        return table.at[pl.ds(2 * half, 2)]

    def sides(half, i):
        return part((low_at, ring_ref.at[0], ring_ref.at[1])[i], half)

    def block(facet):
        return blocks_ref.at[pl.ds(facet * TILES, TILES)]

    def t_go(k, source, target, peer):
        go(tables, k, source, target, peer)

    def t_landed(k, where):
        landed(tables, k, where)

    for d in range(1, 8):
        peer = lax.rem(g + d, 8)
        copy = pltpu.make_async_remote_copy(
            src_ref=send.at[peer], dst_ref=recv.at[g], send_sem=a_send.at[d],
            recv_sem=a_recv.at[g], device_id=(f, peer, c), device_id_type=MESH,
        )
        copy.start()
        started.append(copy)
    t_go(0, part(tab, 0), sides(0, 0), up)
    t_go(1, part(tab, 1), sides(1, 1), down)
    t_go(2, part(tab, 1), sides(1, 0), up)
    t_go(3, part(tab, 0), sides(0, 1), down)
    t_go(4, part(tab, 0), part(flip_at, 0), beside)
    t_go(5, part(tab, 1), part(flip_at, 1), across)
    t_go(6, tab, shifted_ref.at[0], following)
    own_tab = pltpu.make_async_copy(tab, own_at, own_sem.at[0])
    own_tab.start()
    recv[g] = send[g]
    for d in range(1, 8):
        peer = lax.rem(g + d, 8)
        pltpu.make_async_remote_copy(
            src_ref=send.at[peer], dst_ref=recv.at[peer], send_sem=a_send.at[d],
            recv_sem=a_recv.at[peer], device_id=(f, peer, c), device_id_type=MESH,
        ).wait_recv()

    extra = [jnp.zeros((16, SU), F32) for _ in range(3)]
    for b in range(8):
        stage[b] = recv[b, 0]
        misc = recv[b, 1].astype(F32)
        for k in range(2):
            here = rows == 2 * b + k
            for e in range(3):
                line = 3 * k + e
                extra[e] = jnp.where(here, misc[line : line + 1], extra[e])
    for e in range(3):
        stage[8 + e] = extra[e].astype(BF16)
    peers = (far, flip(far), flip(high), high, flip(low), low, flip(f))
    for k, facet in enumerate(peers):
        go(visits, k, stage, block(f), (facet, g, c))
    own_blocks = pltpu.make_async_copy(stage, block(f), own_sem.at[1])
    own_blocks.start()

    t_landed(0, sides(0, 0))
    t_go(7, sides(0, 0), sides(0, 2), up)
    t_go(10, part(low_at, 0), part(flip_low_at, 0), across)
    t_landed(1, sides(1, 1))
    t_go(8, sides(1, 1), sides(1, 2), down)
    t_landed(4, part(flip_at, 0))
    t_landed(5, part(flip_at, 1))
    t_go(9, flip_at, shifted_ref.at[1], following)
    t_landed(2, sides(1, 0))
    t_go(11, part(low_at, 1), part(flip_low_at, 1), across)
    t_go(12, low_at, shifted_ref.at[2], following)
    t_landed(10, part(flip_low_at, 0))
    t_go(13, part(flip_low_at, 0), part(shifted_ref.at[3], 0), following)
    t_landed(11, part(flip_low_at, 1))
    t_go(14, part(flip_low_at, 1), part(shifted_ref.at[3], 1), following)
    sources = (far, flip(far), flip(low), low, flip(high), high, flip(f))
    for k, facet in enumerate(sources):
        landed(visits, k, block(facet))
    t_landed(3, sides(0, 1))
    t_landed(6, shifted_ref.at[0])
    t_landed(7, sides(0, 2))
    t_landed(8, sides(1, 2))
    t_landed(9, shifted_ref.at[1])
    t_landed(12, shifted_ref.at[2])
    t_landed(13, part(shifted_ref.at[3], 0))
    t_landed(14, part(shifted_ref.at[3], 1))
    own_constants.wait()
    own_tab.wait()
    own_blocks.wait()
    for copy in started:
        copy.wait_send()


def sine_of_turns(turns):
    part = turns - jnp.floor(turns + 0.5)
    part = jnp.maximum(jnp.minimum(part, 0.5 - part), -0.5 - part)
    angle = part * (2.0 * math.pi)
    square = angle * angle
    total = jnp.full_like(angle, -1.0 / math.factorial(11))
    for power in (9, 7, 5, 3, 1):
        sign = 1.0 if power % 4 == 1 else -1.0
        total = total * square + sign / math.factorial(power)
    return total * angle


def grid_kernel(
    blocks_ref, planes, gains_ref, vis, line_u, line_v, order_v, order, turned, spots, sems,
):
    f = lax.axis_index("facet")
    g = lax.axis_index("bl")
    c = lax.axis_index("chan")
    sub = lax.broadcasted_iota(jnp.int32, (SU, SU), 0)
    lane = lax.broadcasted_iota(jnp.int32, (SU, SU), 1)
    label = jnp.concatenate([blocks_ref[TILES * i + 10] for i in range(8)], axis=0)
    label = label.astype(F32).astype(jnp.int32) - 1
    number = (label >> 3) * 2 + jnp.where((label & 7) == g, 0, 1)
    number = jnp.where(label >= 0, number, 16).astype(F32)
    across = number.T
    ahead = (across < number) | ((across == number) & (lane < sub))
    place = jnp.sum(jnp.where(ahead, 1.0, 0.0), axis=1, keepdims=True)
    hit = place == lane.astype(F32)
    lines = [
        jnp.sum(jnp.where(hit, sub.astype(F32), 0.0), axis=0, keepdims=True),
        jnp.sum(jnp.where(hit, number, 0.0), axis=0, keepdims=True),
        jnp.sum(jnp.where(number < 16.0, 1.0, 0.0), axis=0, keepdims=True),
        jnp.zeros((5, SU), F32),
    ]
    order_v[...] = jnp.concatenate(lines, axis=0).astype(jnp.int32)
    orders = pltpu.make_async_copy(order_v, order, sems.at[0])
    orders.start()

    for i in range(8):
        line_u[16 * i : 16 * i + 16] = blocks_ref[TILES * i + 8].astype(F32)
        line_v[16 * i : 16 * i + 16] = blocks_ref[TILES * i + 9].astype(F32)
        for b in range(8):
            both = blocks_ref[TILES * i + b].astype(F32)
            vis[16 * i + 2 * b] = both[:8]
            vis[16 * i + 2 * b + 1] = both[8:]
    planes[...] = jnp.zeros_like(planes)
    lines = blocks_ref[8 * TILES].astype(F32)
    off_u, off_v = lines[0:1], lines[1:2]
    dir_l, dir_m, gain_u, gain_v = [
        lines[k : k + 1] + lines[k + 1 : k + 2] + lines[k + 2 : k + 3] for k in (2, 5, 8, 11)
    ]
    tall = (64, SU)
    mine = lax.broadcasted_iota(jnp.int32, tall, 1) == lax.broadcasted_iota(jnp.int32, tall, 0) + c * 64
    along_j = jnp.sum(jnp.where(mine, gain_u, 0.0), axis=1, keepdims=True)
    gains_ref[...] = along_j * gain_v * NORM
    orders.wait()
    count = order[2, 0]
    padded = (count + 3) // 4 * 4

    row = lax.broadcasted_iota(jnp.int32, (8, SU), 0)
    even = (row & 1) == 0
    channel = (c * 4 + (row >> 1)).astype(F32)
    scale = 1.0 + 0.01 * (channel - 0.5 * (CH - 1))

    def swap(pair):
        return jnp.where(even, pltpu.roll(pair, 7, 0), pltpu.roll(pair, 1, 0))

    def prepare(first, size):
        for q in range(size):
            at = first + q
            slot = order[0, at]
            u = line_u[pl.ds(slot, 1), :]
            v = line_v[pl.ds(slot, 1), :]
            along = jnp.where(even, scale * u - off_u, scale * v - off_v)
            spots[at] = along * ROOT
            turns = (scale * (u * dir_l + v * dir_m)) * (1.0 / SU)
            turns = turns - jnp.floor(turns + 0.5)
            wave = sine_of_turns(turns + jnp.where(even, 0.25, 0.0))
            data = vis[slot]
            straight = data * wave
            crossed = data * swap(wave)
            turned[at] = jnp.where(even, straight - swap(straight), crossed + swap(crossed))

    def every(work):
        start = jnp.int32(0)
        for size in (32, 16, 8, 4):
            times = padded // 32 if size == 32 else padded // size % 2

            def one(step, carry, start=start, size=size):
                work(start + step * size, size)
                return carry

            lax.fori_loop(0, times, one, 0)
            start = start + times * size

    every(prepare)

    cells = sub.astype(F32) * ROOT

    def profile(line):
        apart = line - cells
        return jnp.exp2(-(apart * apart)).astype(BF16)

    def gather(first, size):
        for q in range(size):
            at = first + q
            along_u, real, imag = [], [], []
            for ch in range(4):
                along_u.append(profile(spots[at, 2 * ch : 2 * ch + 1, :]))
                along_v = profile(spots[at, 2 * ch + 1 : 2 * ch + 2, :])
                for line, parts in ((2 * ch, real), (2 * ch + 1, imag)):
                    weight = jnp.broadcast_to(turned[at, line : line + 1, :], (16, SU)).astype(BF16)
                    parts.append((along_v.reshape(8, 16, SU) * weight[None]).reshape(SU, SU))
            left = jnp.concatenate(along_u, axis=1)
            right = jnp.concatenate(
                [jnp.concatenate(real, axis=1), jnp.concatenate(imag, axis=1)], axis=0
            )
            planes[order[1, at]] += lax.dot_general(
                left, right, (((1,), (1,)), ((), ())), preferred_element_type=F32
            )

    every(gather)


def finish_kernel(
    sums_ref, gains_ref, near, ring, shifted, beside, after, both_ways, out_ref, parts, give, came, sems,
):
    f = lax.axis_index("facet")
    g = lax.axis_index("bl")
    c = lax.axis_index("chan")
    partner = (f, g, 1 - c)
    barrier = pltpu.get_barrier_semaphore()
    pl.semaphore_signal(barrier, inc=1, device_id=partner, device_id_type=MESH)
    def turn(re, im):
        return jnp.concatenate(
            [jnp.concatenate([re, im], axis=1), jnp.concatenate([-im, re], axis=1)], axis=0
        )

    side = (f // 4) * 4
    y = lax.rem(f, 4)
    low, high, far = [side + lax.rem(y + d, 4) for d in (3, 1, 2)]

    def flip(facet):
        return lax.rem(facet + 4, 8)

    planes = []
    for shift, ends, round_y, flipped in ((0, near, ring, beside), (1, shifted, after, both_ways)):
        for facet, table in (
            (f, ends.at[0]), (flip(f), ends.at[1]), (low, ends.at[2]), (flip(low), ends.at[3]),
            (high, round_y.at[0]), (far, round_y.at[1]),
            (flip(high), flipped.at[0]), (flip(far), flipped.at[1]),
        ):
            planes.append((2 * facet + shift, table))
    for k, (plane, table) in enumerate(planes):
        parts[k] = jnp.dot(
            sums_ref[plane].astype(BF16), turn(table[2], table[3]), preferred_element_type=F32
        ).astype(BF16)

    def rows_of(half):
        rows = pl.ds(pl.multiple_of(half * 64, 64), 64)
        total = jnp.zeros((SU, 2 * SU), F32)
        for k in range(0, 16, 2):
            tall = [
                jnp.concatenate([table[0, rows], table[1, rows]], axis=0)
                for _, table in planes[k : k + 2]
            ]
            total = total + jnp.dot(
                jnp.concatenate(tall, axis=1),
                parts[k : k + 2].reshape(2 * SU, 2 * SU),
                preferred_element_type=F32,
            )
        return jnp.concatenate(
            [total[:64, :SU] - total[64:, SU:], total[:64, SU:] + total[64:, :SU]], axis=1
        )

    give[...] = rows_of(1 - c).astype(BF16)
    pl.semaphore_wait(barrier, 1)
    copy = pltpu.make_async_remote_copy(
        src_ref=give, dst_ref=came, send_sem=sems.at[0], recv_sem=sems.at[1],
        device_id=partner, device_id_type=MESH,
    )
    copy.start()
    keep = rows_of(c)
    both = jnp.concatenate([gains_ref[...], gains_ref[...]], axis=1)
    copy.wait()
    out_ref[...] = (keep + came[...].astype(F32)) * both


def body(
    visibilities, coords, plane_index, block_group, offsets, facet_centre, tables, antenna_gain
):
    held = visibilities.shape[0]
    vmem = pl.BlockSpec(memory_space=pltpu.VMEM)
    hbm = pl.BlockSpec(memory_space=pltpu.HBM)
    loose = pl.BlockSpec(memory_space=pl.ANY)
    dma = pltpu.SemaphoreType.DMA
    two = jax.ShapeDtypeStruct((2, 4, SU, SU), BF16)
    four = jax.ShapeDtypeStruct((4, 4, SU, SU), BF16)
    blocks, near, ring, shifted = pl.pallas_call(
        route_kernel,
        out_shape=(jax.ShapeDtypeStruct((8 * TILES + 1, 16, SU), BF16), four, two, four),
        in_specs=[hbm] * 8,
        out_specs=(loose,) * 4,
        scratch_shapes=[
            pltpu.VMEM((held, 8, SU), BF16),
            pltpu.VMEM((held, 2, SU), BF16),
            pltpu.SMEM((held,), jnp.int32),
            pltpu.SMEM((held,), jnp.int32),
            pltpu.VMEM((2, 2 * SU, SU), BF16),
            pltpu.SMEM((8, 2, 8), jnp.int32),
            pltpu.SMEM((2, 8), F32),
            pltpu.VMEM((1, 2, SU), F32),
            pltpu.VMEM((1, 16, SU), BF16),
            pltpu.VMEM((8, 2, 16, SU), BF16),
            pltpu.VMEM((8, 2, 16, SU), BF16),
            pltpu.VMEM((TILES, 16, SU), BF16),
            pltpu.VMEM((4, SU, SU), BF16),
            dma((8,)), dma((8,)), dma((15,)), dma((15,)), dma((7,)), dma((7,)), dma((8,)),
        ],
        compiler_params=pltpu.CompilerParams(
            collective_id=0, has_side_effects=True, vmem_limit_bytes=58 * 2**20
        ),
        name="route",
    )(
        visibilities.reshape(held, 8, SU), coords, plane_index, block_group.reshape(held),
        tables.reshape(2, 2 * SU, SU), offsets.transpose(0, 2, 1), facet_centre.T, antenna_gain,
    )
    axes = ("facet", "bl", "chan")
    devices = [(f, g, c) for f in range(8) for g in range(8) for c in range(2)]

    def number(f, g, c):
        return (f * 8 + g) * 2 + c

    def moved(array, facets, groups, chans):
        pairs = [
            (number(f, g, c), number((f + facets) % 8, (g + groups) % 8, (c + chans) % 2))
            for f, g, c in devices
        ]
        return lax.ppermute(array, axes, pairs)

    others = [moved(ring, *way) for way in ((4, 0, 0), (0, 1, 0), (4, 1, 1))]
    sums, gains = pl.pallas_call(
        grid_kernel,
        out_shape=(
            jax.ShapeDtypeStruct((17, SU, 2 * SU), F32),
            jax.ShapeDtypeStruct((64, SU), F32),
        ),
        in_specs=[vmem],
        out_specs=(vmem, vmem),
        scratch_shapes=[
            pltpu.VMEM((128, 8, SU), F32),
            pltpu.VMEM((128, SU), F32),
            pltpu.VMEM((128, SU), F32),
            pltpu.VMEM((8, SU), jnp.int32),
            pltpu.SMEM((8, SU), jnp.int32),
            pltpu.VMEM((128, 8, SU), F32),
            pltpu.VMEM((128, 8, SU), F32),
            dma((1,)),
        ],
        compiler_params=pltpu.CompilerParams(vmem_limit_bytes=40 * 2**20),
        cost_estimate=pl.CostEstimate(
            flops=5 * 10**9, bytes_accessed=2 * 10**6, transcendentals=10**7
        ),
        name="grid",
    )(blocks)
    rows_sum = pl.pallas_call(
        finish_kernel,
        out_shape=jax.ShapeDtypeStruct((64, 2 * SU), F32),
        in_specs=[vmem] * 8,
        out_specs=vmem,
        scratch_shapes=[
            pltpu.VMEM((16, SU, 2 * SU), BF16),
            pltpu.VMEM((64, 2 * SU), BF16),
            pltpu.VMEM((64, 2 * SU), BF16),
            dma((2,)),
        ],
        compiler_params=pltpu.CompilerParams(
            collective_id=1, has_side_effects=True, vmem_limit_bytes=24 * 2**20
        ),
        name="finish",
    )(sums, gains, near, ring, shifted, *others)
    return rows_sum.reshape(1, 1, 64, 2, SU)


def solution(mesh):
    in_specs = (
        P(("facet", "bl"), "chan", None, None),
        P(("facet", "bl"), None, None),
        P(("facet", "bl")),
        P(("facet", "bl"), None),
        P(),
        P(),
        P(("facet", "bl"), None, None, None, None),
        P("bl", None, None),
    )
    out_specs = P("facet", "bl", "chan", None, None)
    return jax.shard_map(body, mesh=mesh, in_specs=in_specs, out_specs=out_specs, check_vma=False)
```

```python
import math

import jax
import jax.numpy as jnp
from jax import lax
from jax.experimental import pallas as pl
from jax.experimental.pallas import tpu as pltpu
from jax.sharding import PartitionSpec as P

SU = 128
CH = 8
NORM = SU / math.sqrt(128 * 8 * 8 * CH)
SPREAD = 1.5
ROOT = math.sqrt(math.log2(math.e) / (2.0 * SPREAD * SPREAD))
MESH = pl.DeviceIdType.MESH
F32 = jnp.float32
BF16 = jnp.bfloat16
TILES = 11


def route_kernel(
    vis_hbm, coord_hbm, plane_hbm, group_hbm, raw_hbm, offsets_hbm, centre_hbm, gain_hbm,
    blocks_ref, near_ref, ring_ref, shifted_ref,
    vis_ref, coord_ref, plane_s, group_s, raw_ref, offsets_s, centre_s, gain, constants,
    send, recv, stage, tab, a_send, a_recv, t_send, t_recv, v_send, v_recv, own_sem,
):
    f = lax.axis_index("facet")
    g = lax.axis_index("bl")
    c = lax.axis_index("chan")
    side = (f // 4) * 4
    y = lax.rem(f, 4)
    low = side + lax.rem(y + 3, 4)
    high = side + lax.rem(y + 1, 4)
    far = side + lax.rem(y + 2, 4)

    def flip(facet):
        return lax.rem(facet + 4, 8)

    up, down = (high, g, c), (low, g, c)
    beside, across = (flip(f), g, c), (flip(f), g, 1 - c)
    following = (f, lax.rem(g + 1, 8), c)

    barrier = pltpu.get_barrier_semaphore()
    for d in range(1, 8):
        for peer in ((f, lax.rem(g + d, 8), c), (lax.rem(f + d, 8), g, c)):
            pl.semaphore_signal(barrier, inc=1, device_id=peer, device_id_type=MESH)
    pl.semaphore_signal(barrier, inc=1, device_id=across, device_id_type=MESH)

    fetch_raw = pltpu.make_async_copy(raw_hbm, raw_ref, own_sem.at[2])
    fetch_raw.start()
    names = [
        pltpu.make_async_copy(group_hbm, group_s, own_sem.at[1]),
        pltpu.make_async_copy(plane_hbm, plane_s, own_sem.at[0]),
        pltpu.make_async_copy(vis_hbm, vis_ref, own_sem.at[3]),
        pltpu.make_async_copy(coord_hbm, coord_ref, own_sem.at[4]),
        pltpu.make_async_copy(offsets_hbm, offsets_s, own_sem.at[5]),
        pltpu.make_async_copy(centre_hbm, centre_s, own_sem.at[6]),
        pltpu.make_async_copy(gain_hbm, gain, own_sem.at[7]),
    ]
    for copy in names:
        copy.start()

    wide = (2 * SU, 2 * SU)
    to = lax.broadcasted_iota(jnp.int32, wide, 0)
    source = jnp.where(to < SU, 2 * to, 2 * to - (2 * SU - 1))
    pick = (source == lax.broadcasted_iota(jnp.int32, wide, 1)).astype(F32).astype(BF16)
    fetch_raw.wait()
    first = lax.dot_general(
        raw_ref[0], pick, (((0,), (1,)), ((), ())), preferred_element_type=F32
    ).astype(BF16)
    second = jnp.dot(pick, raw_ref[1], preferred_element_type=F32).astype(BF16)
    tab[0], tab[1] = first[:, :SU], first[:, SU:]
    tab[2], tab[3] = second[:SU], second[SU:]

    for copy in names:
        copy.wait()
    labels = [group_s[n] for n in range(8)]
    rows = lax.broadcasted_iota(jnp.int32, (16, SU), 0)

    def build(group, carry):
        zero = jnp.int32(0)
        i0, i1, n0, n1 = zero, zero, zero, zero
        for n in reversed(range(8)):
            match = labels[n] == group
            i1 = jnp.where(match, i0, i1)
            n1 = jnp.where(match, n0, n1)
            i0 = jnp.where(match, n, i0)
            n0 = jnp.where(match, 1, n0)
        one = vis_ref[i0].astype(F32) * n0.astype(F32)
        two = vis_ref[i1].astype(F32) * n1.astype(F32)
        send[group, 0] = jnp.concatenate([one, two], axis=0).astype(BF16)
        misc = jnp.zeros((16, SU), F32)
        for k, at, here in ((0, i0, n0), (1, i1, n1)):
            spot = coord_ref[at].astype(F32)
            misc = jnp.where(rows == 3 * k, spot[0:1], misc)
            misc = jnp.where(rows == 3 * k + 1, spot[1:2], misc)
            misc = jnp.where(rows == 3 * k + 2, ((plane_s[at] + 1) * here).astype(F32), misc)
        send[group, 1] = misc.astype(BF16)
        return carry

    lax.fori_loop(0, 8, build, 0)

    def line(value):
        return jnp.full((1, SU), value, F32)

    lines = [line(offsets_s[f, k, g].astype(F32)) for k in range(2)]
    for value in (line(centre_s[0, f]), line(centre_s[1, f]), gain[0, 0:1], gain[0, 1:2]):
        for _ in range(3):
            term = value.astype(BF16).astype(F32)
            lines.append(term)
            value = value - term
    lines.append(jnp.zeros((2, SU), F32))
    constants[0] = jnp.concatenate(lines, axis=0).astype(BF16)
    own_constants = pltpu.make_async_copy(constants, blocks_ref.at[pl.ds(88, 1)], own_sem.at[5])
    own_constants.start()
    pl.semaphore_wait(barrier, 15)

    def remote(sems, k, src, dst, peer):
        return pltpu.make_async_remote_copy(
            src_ref=src, dst_ref=dst, send_sem=sems[0].at[k], recv_sem=sems[1].at[k],
            device_id=peer, device_id_type=MESH,
        )

    started = []

    def go(sems, k, src, dst, peer):
        copy = remote(sems, k, src, dst, peer)
        copy.start()
        started.append(copy)

    def landed(sems, k, where):
        remote(sems, k, where, where, up).wait_recv()

    tables, visits = (t_send, t_recv), (v_send, v_recv)

    own_at, flip_at, low_at, flip_low_at = [near_ref.at[i] for i in range(4)]

    def part(table, half):
        return table.at[pl.ds(2 * half, 2)]

    def sides(half, i):
        return part((low_at, ring_ref.at[0], ring_ref.at[1])[i], half)

    def block(facet):
        return blocks_ref.at[pl.ds(facet * TILES, TILES)]

    def t_go(k, source, target, peer):
        go(tables, k, source, target, peer)

    def t_landed(k, where):
        landed(tables, k, where)

    for d in range(1, 8):
        peer = lax.rem(g + d, 8)
        copy = pltpu.make_async_remote_copy(
            src_ref=send.at[peer], dst_ref=recv.at[g], send_sem=a_send.at[d],
            recv_sem=a_recv.at[g], device_id=(f, peer, c), device_id_type=MESH,
        )
        copy.start()
        started.append(copy)
    t_go(0, part(tab, 0), sides(0, 0), up)
    t_go(1, part(tab, 1), sides(1, 1), down)
    t_go(2, part(tab, 1), sides(1, 0), up)
    t_go(3, part(tab, 0), sides(0, 1), down)
    t_go(4, part(tab, 0), part(flip_at, 0), beside)
    t_go(5, part(tab, 1), part(flip_at, 1), across)
    t_go(6, tab, shifted_ref.at[0], following)
    own_tab = pltpu.make_async_copy(tab, own_at, own_sem.at[0])
    own_tab.start()
    recv[g] = send[g]
    for d in range(1, 8):
        peer = lax.rem(g + d, 8)
        pltpu.make_async_remote_copy(
            src_ref=send.at[peer], dst_ref=recv.at[peer], send_sem=a_send.at[d],
            recv_sem=a_recv.at[peer], device_id=(f, peer, c), device_id_type=MESH,
        ).wait_recv()

    extra = [jnp.zeros((16, SU), F32) for _ in range(3)]
    for b in range(8):
        stage[b] = recv[b, 0]
        misc = recv[b, 1].astype(F32)
        for k in range(2):
            here = rows == 2 * b + k
            for e in range(3):
                line = 3 * k + e
                extra[e] = jnp.where(here, misc[line : line + 1], extra[e])
    for e in range(3):
        stage[8 + e] = extra[e].astype(BF16)
    peers = (far, flip(far), flip(high), high, flip(low), low, flip(f))
    for k, facet in enumerate(peers):
        go(visits, k, stage, block(f), (facet, g, c))
    own_blocks = pltpu.make_async_copy(stage, block(f), own_sem.at[1])
    own_blocks.start()

    t_landed(0, sides(0, 0))
    t_go(7, sides(0, 0), sides(0, 2), up)
    t_go(10, part(low_at, 0), part(flip_low_at, 0), across)
    t_landed(1, sides(1, 1))
    t_go(8, sides(1, 1), sides(1, 2), down)
    t_landed(4, part(flip_at, 0))
    t_landed(5, part(flip_at, 1))
    t_go(9, flip_at, shifted_ref.at[1], following)
    t_landed(2, sides(1, 0))
    t_go(11, part(low_at, 1), part(flip_low_at, 1), across)
    t_go(12, low_at, shifted_ref.at[2], following)
    t_landed(10, part(flip_low_at, 0))
    t_go(13, part(flip_low_at, 0), part(shifted_ref.at[3], 0), following)
    t_landed(11, part(flip_low_at, 1))
    t_go(14, part(flip_low_at, 1), part(shifted_ref.at[3], 1), following)
    sources = (far, flip(far), flip(low), low, flip(high), high, flip(f))
    for k, facet in enumerate(sources):
        landed(visits, k, block(facet))
    t_landed(3, sides(0, 1))
    t_landed(6, shifted_ref.at[0])
    t_landed(7, sides(0, 2))
    t_landed(8, sides(1, 2))
    t_landed(9, shifted_ref.at[1])
    t_landed(12, shifted_ref.at[2])
    t_landed(13, part(shifted_ref.at[3], 0))
    t_landed(14, part(shifted_ref.at[3], 1))
    own_constants.wait()
    own_tab.wait()
    own_blocks.wait()
    for copy in started:
        copy.wait_send()


def sine_of_turns(turns):
    part = turns - jnp.floor(turns + 0.5)
    part = jnp.maximum(jnp.minimum(part, 0.5 - part), -0.5 - part)
    angle = part * (2.0 * math.pi)
    square = angle * angle
    total = jnp.full_like(angle, -1.0 / math.factorial(11))
    for power in (9, 7, 5, 3, 1):
        sign = 1.0 if power % 4 == 1 else -1.0
        total = total * square + sign / math.factorial(power)
    return total * angle


def grid_kernel(
    blocks_ref, planes, gains_ref, vis, line_u, line_v, order_v, order, sems,
):
    f = lax.axis_index("facet")
    g = lax.axis_index("bl")
    c = lax.axis_index("chan")
    sub = lax.broadcasted_iota(jnp.int32, (SU, SU), 0)
    lane = lax.broadcasted_iota(jnp.int32, (SU, SU), 1)
    label = jnp.concatenate([blocks_ref[TILES * i + 10] for i in range(8)], axis=0)
    label = label.astype(F32).astype(jnp.int32) - 1
    number = (label >> 3) * 2 + jnp.where((label & 7) == g, 0, 1)
    number = jnp.where(label >= 0, number, 16).astype(F32)
    across = number.T
    ahead = (across < number) | ((across == number) & (lane < sub))
    place = jnp.sum(jnp.where(ahead, 1.0, 0.0), axis=1, keepdims=True)
    hit = place == lane.astype(F32)
    lines = [
        jnp.sum(jnp.where(hit, sub.astype(F32), 0.0), axis=0, keepdims=True),
        jnp.sum(jnp.where(hit, number, 0.0), axis=0, keepdims=True),
        jnp.sum(jnp.where(number < 16.0, 1.0, 0.0), axis=0, keepdims=True),
        jnp.zeros((5, SU), F32),
    ]
    order_v[...] = jnp.concatenate(lines, axis=0).astype(jnp.int32)
    orders = pltpu.make_async_copy(order_v, order, sems.at[0])
    orders.start()

    for i in range(8):
        line_u[16 * i : 16 * i + 16] = blocks_ref[TILES * i + 8].astype(F32)
        line_v[16 * i : 16 * i + 16] = blocks_ref[TILES * i + 9].astype(F32)
        for b in range(8):
            both = blocks_ref[TILES * i + b].astype(F32)
            vis[16 * i + 2 * b] = both[:8]
            vis[16 * i + 2 * b + 1] = both[8:]
    planes[...] = jnp.zeros_like(planes)
    lines = blocks_ref[8 * TILES].astype(F32)
    off_u, off_v = lines[0:1], lines[1:2]
    dir_l, dir_m, gain_u, gain_v = [
        lines[k : k + 1] + lines[k + 1 : k + 2] + lines[k + 2 : k + 3] for k in (2, 5, 8, 11)
    ]
    tall = (64, SU)
    mine = lax.broadcasted_iota(jnp.int32, tall, 1) == lax.broadcasted_iota(jnp.int32, tall, 0) + c * 64
    along_j = jnp.sum(jnp.where(mine, gain_u, 0.0), axis=1, keepdims=True)
    gains_ref[...] = along_j * gain_v * NORM
    orders.wait()
    count = order[2, 0]
    padded = (count + 3) // 4 * 4

    row = lax.broadcasted_iota(jnp.int32, (8, SU), 0)
    even = (row & 1) == 0
    channel = (c * 4 + (row >> 1)).astype(F32)
    scale = 1.0 + 0.01 * (channel - 0.5 * (CH - 1))

    def swap(pair):
        return jnp.where(even, pltpu.roll(pair, 7, 0), pltpu.roll(pair, 1, 0))

    def prepare(slot):
        u = line_u[pl.ds(slot, 1), :]
        v = line_v[pl.ds(slot, 1), :]
        along = jnp.where(even, scale * u - off_u, scale * v - off_v)
        turns = (scale * (u * dir_l + v * dir_m)) * (1.0 / SU)
        turns = turns - jnp.floor(turns + 0.5)
        wave = sine_of_turns(turns + jnp.where(even, 0.25, 0.0))
        data = vis[slot]
        straight = data * wave
        crossed = data * swap(wave)
        return along * ROOT, jnp.where(even, straight - swap(straight), crossed + swap(crossed))

    def every(work):
        start = jnp.int32(0)
        for size in (64, 32, 16, 8, 4):
            times = padded // 64 if size == 64 else padded // size % 2

            def one(step, carry, start=start, size=size):
                work(start + step * size, size)
                return carry

            lax.fori_loop(0, times, one, 0)
            start = start + times * size

    cells = sub.astype(F32) * ROOT

    def profile(line):
        apart = line - cells
        return jnp.exp2(-(apart * apart)).astype(BF16)

    def gather(first, size):
        for q in range(size):
            at = first + q
            spots, turned = prepare(order[0, at])
            along_u, real, imag = [], [], []
            for ch in range(4):
                along_u.append(profile(spots[2 * ch : 2 * ch + 1]))
                along_v = profile(spots[2 * ch + 1 : 2 * ch + 2])
                for line, parts in ((2 * ch, real), (2 * ch + 1, imag)):
                    weight = jnp.broadcast_to(turned[line : line + 1], (16, SU)).astype(BF16)
                    parts.append((along_v.reshape(8, 16, SU) * weight[None]).reshape(SU, SU))
            left = jnp.concatenate(along_u, axis=1)
            right = jnp.concatenate(
                [jnp.concatenate(real, axis=1), jnp.concatenate(imag, axis=1)], axis=0
            )
            planes[order[1, at]] += lax.dot_general(
                left, right, (((1,), (1,)), ((), ())), preferred_element_type=F32
            )

    every(gather)


def finish_kernel(
    sums_ref, gains_ref, near, ring, shifted, beside, after, both_ways, out_ref, parts, give, came, sems,
):
    f = lax.axis_index("facet")
    g = lax.axis_index("bl")
    c = lax.axis_index("chan")
    partner = (f, g, 1 - c)
    barrier = pltpu.get_barrier_semaphore()
    pl.semaphore_signal(barrier, inc=1, device_id=partner, device_id_type=MESH)
    def turn(re, im):
        return jnp.concatenate(
            [jnp.concatenate([re, im], axis=1), jnp.concatenate([-im, re], axis=1)], axis=0
        )

    side = (f // 4) * 4
    y = lax.rem(f, 4)
    low, high, far = [side + lax.rem(y + d, 4) for d in (3, 1, 2)]

    def flip(facet):
        return lax.rem(facet + 4, 8)

    planes = []
    for shift, ends, round_y, flipped in ((0, near, ring, beside), (1, shifted, after, both_ways)):
        for facet, table in (
            (f, ends.at[0]), (flip(f), ends.at[1]), (low, ends.at[2]), (flip(low), ends.at[3]),
            (high, round_y.at[0]), (far, round_y.at[1]),
            (flip(high), flipped.at[0]), (flip(far), flipped.at[1]),
        ):
            planes.append((2 * facet + shift, table))
    for k, (plane, table) in enumerate(planes):
        parts[k] = jnp.dot(
            sums_ref[plane].astype(BF16), turn(table[2], table[3]), preferred_element_type=F32
        ).astype(BF16)

    def rows_of(half):
        rows = pl.ds(pl.multiple_of(half * 64, 64), 64)
        total = jnp.zeros((SU, 2 * SU), F32)
        for k in range(0, 16, 2):
            tall = [
                jnp.concatenate([table[0, rows], table[1, rows]], axis=0)
                for _, table in planes[k : k + 2]
            ]
            total = total + jnp.dot(
                jnp.concatenate(tall, axis=1),
                parts[k : k + 2].reshape(2 * SU, 2 * SU),
                preferred_element_type=F32,
            )
        return jnp.concatenate(
            [total[:64, :SU] - total[64:, SU:], total[:64, SU:] + total[64:, :SU]], axis=1
        )

    give[...] = rows_of(1 - c).astype(BF16)
    pl.semaphore_wait(barrier, 1)
    copy = pltpu.make_async_remote_copy(
        src_ref=give, dst_ref=came, send_sem=sems.at[0], recv_sem=sems.at[1],
        device_id=partner, device_id_type=MESH,
    )
    copy.start()
    keep = rows_of(c)
    both = jnp.concatenate([gains_ref[...], gains_ref[...]], axis=1)
    copy.wait()
    out_ref[...] = (keep + came[...].astype(F32)) * both


def body(
    visibilities, coords, plane_index, block_group, offsets, facet_centre, tables, antenna_gain
):
    held = visibilities.shape[0]
    vmem = pl.BlockSpec(memory_space=pltpu.VMEM)
    hbm = pl.BlockSpec(memory_space=pltpu.HBM)
    loose = pl.BlockSpec(memory_space=pl.ANY)
    dma = pltpu.SemaphoreType.DMA
    two = jax.ShapeDtypeStruct((2, 4, SU, SU), BF16)
    four = jax.ShapeDtypeStruct((4, 4, SU, SU), BF16)
    blocks, near, ring, shifted = pl.pallas_call(
        route_kernel,
        out_shape=(jax.ShapeDtypeStruct((8 * TILES + 1, 16, SU), BF16), four, two, four),
        in_specs=[hbm] * 8,
        out_specs=(loose,) * 4,
        scratch_shapes=[
            pltpu.VMEM((held, 8, SU), BF16),
            pltpu.VMEM((held, 2, SU), BF16),
            pltpu.SMEM((held,), jnp.int32),
            pltpu.SMEM((held,), jnp.int32),
            pltpu.VMEM((2, 2 * SU, SU), BF16),
            pltpu.SMEM((8, 2, 8), jnp.int32),
            pltpu.SMEM((2, 8), F32),
            pltpu.VMEM((1, 2, SU), F32),
            pltpu.VMEM((1, 16, SU), BF16),
            pltpu.VMEM((8, 2, 16, SU), BF16),
            pltpu.VMEM((8, 2, 16, SU), BF16),
            pltpu.VMEM((TILES, 16, SU), BF16),
            pltpu.VMEM((4, SU, SU), BF16),
            dma((8,)), dma((8,)), dma((15,)), dma((15,)), dma((7,)), dma((7,)), dma((8,)),
        ],
        compiler_params=pltpu.CompilerParams(
            collective_id=0, has_side_effects=True, vmem_limit_bytes=58 * 2**20
        ),
        name="route",
    )(
        visibilities.reshape(held, 8, SU), coords, plane_index, block_group.reshape(held),
        tables.reshape(2, 2 * SU, SU), offsets.transpose(0, 2, 1), facet_centre.T, antenna_gain,
    )
    axes = ("facet", "bl", "chan")
    devices = [(f, g, c) for f in range(8) for g in range(8) for c in range(2)]

    def number(f, g, c):
        return (f * 8 + g) * 2 + c

    def moved(array, facets, groups, chans):
        pairs = [
            (number(f, g, c), number((f + facets) % 8, (g + groups) % 8, (c + chans) % 2))
            for f, g, c in devices
        ]
        return lax.ppermute(array, axes, pairs)

    others = [moved(ring, *way) for way in ((4, 0, 0), (0, 1, 0), (4, 1, 1))]
    sums, gains = pl.pallas_call(
        grid_kernel,
        out_shape=(
            jax.ShapeDtypeStruct((17, SU, 2 * SU), F32),
            jax.ShapeDtypeStruct((64, SU), F32),
        ),
        in_specs=[vmem],
        out_specs=(vmem, vmem),
        scratch_shapes=[
            pltpu.VMEM((128, 8, SU), F32),
            pltpu.VMEM((128, SU), F32),
            pltpu.VMEM((128, SU), F32),
            pltpu.VMEM((8, SU), jnp.int32),
            pltpu.SMEM((8, SU), jnp.int32),
            dma((1,)),
        ],
        compiler_params=pltpu.CompilerParams(vmem_limit_bytes=40 * 2**20),
        cost_estimate=pl.CostEstimate(
            flops=5 * 10**9, bytes_accessed=2 * 10**6, transcendentals=10**7
        ),
        name="grid",
    )(blocks)
    rows_sum = pl.pallas_call(
        finish_kernel,
        out_shape=jax.ShapeDtypeStruct((64, 2 * SU), F32),
        in_specs=[vmem] * 8,
        out_specs=vmem,
        scratch_shapes=[
            pltpu.VMEM((16, SU, 2 * SU), BF16),
            pltpu.VMEM((64, 2 * SU), BF16),
            pltpu.VMEM((64, 2 * SU), BF16),
            dma((2,)),
        ],
        compiler_params=pltpu.CompilerParams(
            collective_id=1, has_side_effects=True, vmem_limit_bytes=24 * 2**20
        ),
        name="finish",
    )(sums, gains, near, ring, shifted, *others)
    return rows_sum.reshape(1, 1, 64, 2, SU)


def solution(mesh):
    in_specs = (
        P(("facet", "bl"), "chan", None, None),
        P(("facet", "bl"), None, None),
        P(("facet", "bl")),
        P(("facet", "bl"), None),
        P(),
        P(),
        P(("facet", "bl"), None, None, None, None),
        P("bl", None, None),
    )
    out_specs = P("facet", "bl", "chan", None, None)
    return jax.shard_map(body, mesh=mesh, in_specs=in_specs, out_specs=out_specs, check_vma=False)
```
